256 devices in a mesh: gz: 8 (over x, core), row: 8 (over z), col: 4 (over y).
Axes of the slice: x: 4, y: 4, z: 8, core: 2. Of those that a mesh axis runs over, the one named last changes fastest.
Arguments:
- subtree_lower: bfloat16 [8, 4096, 2048], P('gz', 'row', 'col'), may hold values from -6 to 6
- subtree_upper: bfloat16 [8, 2048, 4096], P('gz', 'col', 'row'), may hold values from -0.125 to 0.125
- touched: int32 [8, 32], P('gz'), may hold values 0 or 1
- front: float32 [4096, 8, 4, 128], P('row', 'gz', 'col'), may hold values from -6 to 96
Outputs:
- lower_panel: float32 [4096, 128], P('row')
- upper_panel: float32 [128, 8, 4, 128], P(None, 'gz', 'col')
- trailing: float32 [4096, 8, 4, 128], P('row', 'gz', 'col')
The draws below stay inside these ranges and needn't reach their ends.
All inputs are finite; a program needn't handle non-finite values. No bound on the sum of `touched` on one device may be relied on, other than what follows from the above.
Results may differ from the reference program's by a relative error of at most 0.0003.
Values may be sent and summed in bfloat16 or wider, within the bound.
A program may use at most 64 MiB of HBM per device.

```python
import jax
import jax.numpy as jnp
from jax import lax

BLOCK = 128
COUPLING = 2048
PANELS = 32
ORDER = 4096
N_GZ = 8
N_COL = 4


def draw_front(key, part):
    key = jax.random.fold_in(key, 7)
    random_key, lifting_key = jax.random.split(key)
    random_part = jnp.clip(jax.random.normal(random_key, (ORDER, ORDER), jnp.float32), -6.0, 6.0)
    lifting = jax.random.uniform(lifting_key, (ORDER,), jnp.float32, 45.0, 90.0)
    diagonal_mask = jnp.arange(ORDER)[:, None] == jnp.arange(ORDER)[None, :]
    whole = random_part + jnp.where(diagonal_mask, lifting[:, None], 0.0)
    return whole.reshape(ORDER, N_GZ, N_COL, BLOCK)


def with_ends(result, stream_key, low, top_value):
    longest = result.shape.index(max(result.shape))
    spots = []
    for shift in (0, 1):
        where = [jax.random.randint(jax.random.fold_in(stream_key, axis), (), 0, length) for axis, length in enumerate(result.shape)]
        where[longest] = (where[longest] + shift) % result.shape[longest]
        spots.append(tuple(where))
    return result.at[spots[0]].set(low).at[spots[1]].set(top_value)


def block_levels(stream_key, dims, pieces, smallest, largest):
    gain = 1.0
    for position, shards_of in pieces:
        heights = jax.random.uniform(jax.random.fold_in(jax.random.fold_in(stream_key, 6), position), (shards_of,), jnp.float32, smallest / len(pieces), largest / len(pieces))
        gain = gain * jnp.repeat(jnp.exp(heights), dims[position] // shards_of).reshape((-1,) + (1,) * (len(dims) - 1 - position))
    return gain


def gaussian(key, shape, deviation, bound, pieces=(), held_as=jnp.bfloat16):
    gain = block_levels(key, shape, pieces, -0.22, 0.18) if pieces else 1.0
    entries = jax.random.normal(key, shape, jnp.float32) * deviation * gain
    return jnp.minimum(jnp.maximum(entries, -bound), bound).astype(held_as)


def setup_inputs(seed: int = 0) -> dict:
    key_of = jax.random.split(jax.random.key(seed), 5)
    subtree_lower = gaussian(key_of[0], (N_GZ, ORDER, COUPLING), 1.0, 6.0, ((0, 8), (1, 8), (2, 4)))
    subtree_upper = gaussian(key_of[1], (N_GZ, COUPLING, ORDER), COUPLING ** -0.5, 0.125, ((0, 8), (1, 4), (2, 8)))
    touched = with_ends((jax.random.randint(key_of[2], (N_GZ, PANELS), 0, 4) < 3).astype(jnp.int32), jax.random.fold_in(key_of[2], 1), 0, 1)
    front = draw_front(jax.random.fold_in(key_of[4], 71), 0)
    return dict(subtree_lower=subtree_lower, subtree_upper=subtree_upper, touched=touched, front=front)


def factor_small(dense_matrix):
    span_length = dense_matrix.shape[0]
    places = jnp.arange(span_length)
    lower_factors = jnp.eye(span_length, dtype=dense_matrix.dtype)
    worked = dense_matrix
    for column_at in range(span_length):
        scaled = jnp.where(places > column_at, worked[:, column_at] / worked[column_at, column_at], jnp.zeros((), dense_matrix.dtype))
        lower_factors = lower_factors + jnp.where(places[None, :] == column_at, scaled[:, None], jnp.zeros((), dense_matrix.dtype))
        worked = worked - scaled[:, None] * worked[column_at, :][None, :]
    return (lower_factors, jnp.triu(worked))

def factor(dense_matrix):
    span_length = dense_matrix.shape[0]
    if span_length <= 16:
        return factor_small(dense_matrix)
    center_block = span_length // 2
    lower_leading, upper_leading = factor(dense_matrix[:center_block, :center_block])
    upper_rightward = lax.linalg.triangular_solve(lower_leading, dense_matrix[:center_block, center_block:], left_side=True, lower=True, unit_diagonal=True)
    lower_beneath = lax.linalg.triangular_solve(upper_leading, dense_matrix[center_block:, :center_block], left_side=False, lower=False)
    remain = dense_matrix[center_block:, center_block:] - jnp.dot(lower_beneath, upper_rightward, precision=lax.Precision.HIGHEST)
    lower_closing, upper_closing = factor(remain)
    blank_blocks = jnp.zeros((center_block, span_length - center_block), dense_matrix.dtype)
    lower_factors = jnp.concatenate([jnp.concatenate([lower_leading, blank_blocks], 1), jnp.concatenate([lower_beneath, lower_closing], 1)], 0)
    upper_factors = jnp.concatenate([jnp.concatenate([upper_leading, upper_rightward], 1), jnp.concatenate([blank_blocks.T, upper_closing], 1)], 0)
    return (lower_factors, upper_factors)

def reference(subtree_lower, subtree_upper, touched, front):
    layer_marks = jnp.repeat(touched.astype(jnp.bfloat16), BLOCK, axis=1)

    def add_layer(running, members):
        lower_part, upper_part, marked = members
        lower_part = lower_part * marked[:, None]
        upper_part = upper_part * marked[None, :]
        return (running + jnp.dot(lower_part.astype(jnp.float32), upper_part.astype(jnp.float32), preferred_element_type=jnp.float32), None)
    schur, _ = lax.scan(add_layer, jnp.zeros((ORDER, ORDER), jnp.float32), (subtree_lower, subtree_upper, layer_marks))
    updated = front.reshape(ORDER, ORDER) - schur
    lower_diag, upper_diag = factor(updated[:BLOCK, :BLOCK])
    lower_panel = lax.linalg.triangular_solve(upper_diag, updated[:, :BLOCK], left_side=False, lower=False)
    upper_panel = lax.linalg.triangular_solve(lower_diag, updated[:BLOCK, :], left_side=True, lower=True, unit_diagonal=True)
    trailing = updated - jnp.dot(lower_panel, upper_panel, precision=lax.Precision.HIGHEST)
    return (lower_panel, upper_panel.reshape(BLOCK, N_GZ, N_COL, BLOCK), trailing.reshape(ORDER, N_GZ, N_COL, BLOCK))
```

```python
import jax
import jax.numpy as jnp
from jax import lax
from jax.experimental import pallas as pl
from jax.experimental.pallas import tpu as pltpu
from jax.sharding import PartitionSpec as P

BLOCK = 128


def exact_dot(left, right):
    return jnp.dot(
        left, right, precision=lax.Precision.HIGHEST, preferred_element_type=jnp.float32
    )


def eliminate(first, count, worked, product, lower, lower_inverse):
    rows = lax.broadcasted_iota(jnp.int32, (BLOCK, BLOCK), 0)
    lanes = lax.broadcasted_iota(jnp.int32, (BLOCK, BLOCK), 1)

    def step(at, carry):
        dense = worked[...]
        pivot_row = worked[pl.ds(at, 1), :]
        product_row = product[pl.ds(at, 1), :]
        lower_inverse[pl.ds(at, 1), :] = product_row
        column = jnp.sum(jnp.where(lanes == at, dense, 0.0), axis=1, keepdims=True)
        pivot = jnp.sum(
            jnp.where(lanes[:1] == at, pivot_row, 0.0), axis=1, keepdims=True
        )
        scaled = jnp.where(rows == at, 0.0, column / pivot)
        worked[...] = dense - scaled * pivot_row
        product[...] = product[...] - scaled * product_row
        lower[...] = jnp.where((lanes == at) & (rows > at), scaled, lower[...])
        return carry

    lax.fori_loop(first, first + count, step, 0)


def start_elimination(pivot, worked, product, lower):
    rows = lax.broadcasted_iota(jnp.int32, (BLOCK, BLOCK), 0)
    lanes = lax.broadcasted_iota(jnp.int32, (BLOCK, BLOCK), 1)
    identity = jnp.where(rows == lanes, 1.0, 0.0)
    worked[...] = pivot
    product[...] = identity
    lower[...] = identity


def finish_elimination(worked, product, lower):
    rows = lax.broadcasted_iota(jnp.int32, (BLOCK, BLOCK), 0)
    lanes = lax.broadcasted_iota(jnp.int32, (BLOCK, BLOCK), 1)
    pivots = jnp.sum(jnp.where(rows == lanes, worked[...], 0.0), axis=1, keepdims=True)
    return exact_dot(product[...] / pivots, lower[...])


def factor_kernel(pivot, lower_inverse, upper_inverse, worked, product, lower):
    start_elimination(pivot[...], worked, product, lower)
    eliminate(0, BLOCK, worked, product, lower, lower_inverse)
    upper_inverse[...] = finish_elimination(worked, product, lower)


def factor(pivot):
    square = jax.ShapeDtypeStruct((BLOCK, BLOCK), jnp.float32)
    return pl.pallas_call(
        factor_kernel,
        out_shape=(square, square),
        scratch_shapes=[pltpu.VMEM((BLOCK, BLOCK), jnp.float32)] * 3,
    )(pivot)


def broadcast(shard, axis, root):
    mine = lax.axis_index(axis) == root
    return lax.psum(jnp.where(mine, shard, jnp.zeros_like(shard)), axis)


def shards(subtree_lower, subtree_upper, touched, front):
    local_rows = front.shape[0]
    width = front.shape[3]
    marks = touched[0].astype(jnp.bfloat16)
    own_marks = lax.dynamic_slice_in_dim(
        marks, lax.axis_index("row") * (local_rows // width), local_rows // width
    )
    own_marks = jnp.repeat(own_marks, width)
    lower_kept = subtree_lower[0] * own_marks[:, None]
    upper_kept = subtree_upper[0] * own_marks[None, :]
    first = (
        (lax.axis_index("gz") == 0) & (lax.axis_index("row") == 0) & (lax.axis_index("col") == 0)
    )
    pivot_term = -jnp.dot(
        lower_kept[:width], upper_kept[:, :width], preferred_element_type=jnp.float32
    )
    pivot_term = jnp.where(lax.axis_index("row") == 0, pivot_term, 0.0)
    pivot_term = pivot_term + jnp.where(first, front[:width, 0, 0, :], 0.0)
    lower_inverse, upper_inverse = factor(lax.psum(pivot_term, ("gz", "row", "col")))
    layer_term = jnp.dot(
        lower_kept,
        lax.all_gather(upper_kept, "row", axis=1, tiled=True),
        preferred_element_type=jnp.float32,
    )
    blocks = layer_term.reshape(local_rows, 32, width).transpose(1, 0, 2)
    schur = lax.psum_scatter(blocks, ("gz", "col"), scatter_dimension=0, tiled=False)
    updated = front[:, 0, 0, :] - schur
    lower_panel = broadcast(exact_dot(updated, upper_inverse), ("gz", "col"), 0)
    upper_panel = broadcast(exact_dot(lower_inverse, updated[:width]), "row", 0)
    trailing = updated - exact_dot(lower_panel, upper_panel)
    return (
        lower_panel,
        upper_panel.reshape(width, 1, 1, width),
        trailing.reshape(local_rows, 1, 1, width),
    )


def solution(mesh):
    placed = (
        P("gz", "row", "col"),
        P("gz", "col", "row"),
        P("gz", None),
        P("row", "gz", "col", None),
    )
    return jax.shard_map(
        shards,
        mesh=mesh,
        in_specs=placed,
        out_specs=(P("row", None), P(None, "gz", "col", None), P("row", "gz", "col", None)),
        check_vma=False,
    )
```

```python
import functools

import jax
import jax.numpy as jnp
from jax import lax
from jax.experimental import pallas as pl
from jax.experimental.pallas import tpu as pltpu
from jax.sharding import PartitionSpec as P

BLOCK = 128
MESH = pl.DeviceIdType.MESH
ORDER_OF_K = (0, 1, 3, 2)


def exact_dot(left, right):
    return jnp.dot(
        left, right, precision=lax.Precision.HIGHEST, preferred_element_type=jnp.float32
    )


def eliminate(first, count, worked, product, lower, lower_inverse):
    rows = lax.broadcasted_iota(jnp.int32, (BLOCK, BLOCK), 0)
    lanes = lax.broadcasted_iota(jnp.int32, (BLOCK, BLOCK), 1)

    def step(at, carry):
        dense = worked[...]
        pivot_row = worked[pl.ds(at, 1), :]
        product_row = product[pl.ds(at, 1), :]
        lower_inverse[pl.ds(at, 1), :] = product_row
        column = jnp.sum(jnp.where(lanes == at, dense, 0.0), axis=1, keepdims=True)
        pivot = jnp.sum(
            jnp.where(lanes[:1] == at, pivot_row, 0.0), axis=1, keepdims=True
        )
        scaled = jnp.where(rows == at, 0.0, column / pivot)
        worked[...] = dense - scaled * pivot_row
        product[...] = product[...] - scaled * product_row
        lower[...] = jnp.where((lanes == at) & (rows > at), scaled, lower[...])
        return carry

    lax.fori_loop(first, first + count, step, 0)


def start_elimination(pivot, worked, product, lower):
    rows = lax.broadcasted_iota(jnp.int32, (BLOCK, BLOCK), 0)
    lanes = lax.broadcasted_iota(jnp.int32, (BLOCK, BLOCK), 1)
    identity = jnp.where(rows == lanes, 1.0, 0.0)
    worked[...] = pivot
    product[...] = identity
    lower[...] = identity


def finish_elimination(worked, product, lower):
    rows = lax.broadcasted_iota(jnp.int32, (BLOCK, BLOCK), 0)
    lanes = lax.broadcasted_iota(jnp.int32, (BLOCK, BLOCK), 1)
    pivots = jnp.sum(jnp.where(rows == lanes, worked[...], 0.0), axis=1, keepdims=True)
    return exact_dot(product[...] / pivots, lower[...])


def remote(src, dst, send_sem, recv_sem, **where):
    return pltpu.make_async_remote_copy(
        src_ref=src,
        dst_ref=dst,
        send_sem=send_sem,
        recv_sem=recv_sem,
        device_id=where,
        device_id_type=MESH,
    )


def front_kernel(
    n_gz, n_row, n_col,
    lower_in, upper_in, touched, front,
    lower_panel, upper_panel, trailing,
    lowers, uppers, gathered, terms, arrived,
    first_rows, first_columns, pivot_front, row_front,
    split, split_in, summed, summed_in, row_in, panel, row_panel,
    worked, product, lower_unit, lower_inverse,
    up_send, up_recv, low_send, low_recv, z_send, z_recv, term_send, term_recv,
    chain_send, chain_recv, row_front_sem, split_send, split_recv, summed_send, summed_recv,
    row_send, row_recv, panel_send, panel_recv, spread_send, spread_recv,
):
    g, r, c = lax.axis_index("gz"), lax.axis_index("row"), lax.axis_index("col")
    height = lower_in.shape[0]
    panels = height // BLOCK
    half = height // 2

    def gz(step):
        return lax.rem(g + step, n_gz)

    def row(step):
        return lax.rem(r + n_row + step, n_row)

    def col(step):
        return lax.rem(c + n_col + step, n_col)

    barrier = pltpu.get_barrier_semaphore()
    for step in range(1, n_gz):
        pl.semaphore_signal(barrier, inc=1, device_id={"gz": gz(step)}, device_id_type=MESH)
    for step in range(1, n_row):
        pl.semaphore_signal(barrier, inc=1, device_id={"row": row(step)}, device_id_type=MESH)
    for step in range(1, n_col):
        pl.semaphore_signal(barrier, inc=1, device_id={"col": col(step)}, device_id_type=MESH)

    for at in range(panels):
        mark = touched[0, r * panels + at].astype(jnp.float32)
        span = pl.ds(at * BLOCK, BLOCK)
        uppers[at] = (upper_in[:, span].astype(jnp.float32) * mark).astype(jnp.bfloat16)
        lowers[c, span, :] = (lower_in[span, :].astype(jnp.float32) * mark).astype(jnp.bfloat16)
    gathered[r, c] = uppers[c]

    @pl.when(r == 0)
    def _():
        first_rows[...] = lowers[c, :BLOCK, :]
        first_columns[...] = uppers[0]
        pivot_front[...] = front[:BLOCK, :]

    @pl.when((r == 0) & (g == 0))
    def _():
        row_front[...] = front[:BLOCK, :]

    pl.semaphore_wait(barrier, n_gz + n_row + n_col - 3)

    corner = (g == 0) & (c == 0)

    def chain(way, at):
        slot = 0 if way > 0 else 1
        buffers = (first_columns, first_rows, pivot_front)
        return remote(
            buffers[at], buffers[at], chain_send.at[slot, at], chain_recv.at[at], row=row(way)
        )

    def chain_start(way):
        chain(way, 0).start()
        chain(way, 1).start()

        @pl.when(corner)
        def _():
            chain(way, 2).start()

    def chain_arrive():
        chain(1, 0).wait_recv()
        chain(1, 1).wait_recv()

        @pl.when(corner)
        def _():
            chain(1, 2).wait_recv()

    def chain_sent(way):
        chain(way, 0).wait_send()
        chain(way, 1).wait_send()

        @pl.when(corner)
        def _():
            chain(way, 2).wait_send()

    def row_front_copy():
        return remote(
            front.at[pl.ds(0, BLOCK), :], row_front, row_front_sem.at[0], row_front_sem.at[1], row=g
        )

    def chain_hop(hop):
        @pl.when(r == hop)
        def _():
            chain_arrive()
            if hop < n_row // 2:
                chain_start(1)

        if hop < n_row // 2:
            @pl.when(r == n_row - hop)
            def _():
                chain_arrive()
                if hop < n_row // 2 - 1:
                    chain_start(-1)

    @pl.when(r == 0)
    def _():
        chain_start(1)
        chain_start(-1)

    up_copies = []
    for slot, step in enumerate(ORDER_OF_K[1:]):
        up_copies.append(
            remote(
                uppers.at[col(step)], gathered.at[r, c], up_send.at[slot], up_recv.at[c], col=col(step)
            )
        )

    def up_arrive(step):
        remote(
            uppers.at[0], gathered.at[r, col(step)], up_send.at[0], up_recv.at[col(step)], col=col(step)
        ).wait_recv()

    def z_copy(way, distance, place):
        source = row(-way * distance)
        k_block = col(ORDER_OF_K[place])
        piece = gathered.at[source, k_block]
        slot = 0 if way > 0 else 1
        at = distance * n_col + place
        return remote(piece, piece, z_send.at[slot, at], z_recv.at[source, k_block], row=row(way))

    last = n_row // 2 - 1
    z_order = [(distance, place) for distance in range(last) for place in range(n_col)]
    z_order += [(last, place) for place in range(n_col // 2)]
    z_copies = []

    def z_step(at):
        distance, place = z_order[at]
        if distance == 0 and place > 0:
            up_arrive(ORDER_OF_K[place])
        for way in (1, -1):
            used = place
            if distance == last and way < 0:
                used = place + n_col // 2
            copy = z_copy(way, distance, used)
            if distance > 0:
                copy.wait_recv()
            copy.start()
            z_copies.append(copy)

    def low_copy(way):
        slot = 0 if way > 0 else 1
        return remote(
            lowers.at[c], lowers.at[c], low_send.at[slot], low_recv.at[slot], col=col(way)
        )

    def low_pass(way):
        slot = 0 if way > 0 else 1
        piece = lowers.at[col(-way), pl.ds(slot * half, half), :]
        return remote(piece, piece, low_send.at[2 + slot], low_recv.at[2 + slot], col=col(way))

    def low_wait(way):
        slot = 0 if way > 0 else 1
        block = lowers.at[col(-way)]
        remote(block, block, low_send.at[slot], low_recv.at[slot], col=col(way)).wait_recv()

    def low_far_wait(way):
        slot = 0 if way > 0 else 1
        piece = lowers.at[col(2), pl.ds(slot * half, half), :]
        remote(piece, piece, low_send.at[2 + slot], low_recv.at[2 + slot], col=col(way)).wait_recv()

    for copy in up_copies:
        copy.start()
    z_step(0)
    for way in (1, -1):
        low_copy(way).start()

    @pl.when((r == 0) & (g != 0))
    def _():
        row_front_copy().start()

    for hop in range(1, n_row // 2 + 1):
        chain_hop(hop)
        if hop < n_col:
            z_step(hop)

    column = first_columns[...]
    pivot_part = jnp.dot(first_rows[...], column, preferred_element_type=jnp.float32)
    sums, backs = BLOCK // n_col + BLOCK, BLOCK // n_col
    for at in range(n_col):
        split[at, :backs] = -pivot_part[at * backs : (at + 1) * backs]
        split[at, backs:sums] = -jnp.dot(
            lowers[c, at * BLOCK : (at + 1) * BLOCK, :], column, preferred_element_type=jnp.float32
        )
        split[at, sums:] = -jnp.dot(
            first_rows[...], uppers[at], preferred_element_type=jnp.float32
        )

    @pl.when(corner)
    def _():
        for at in range(n_col):
            split[at, :backs] += pivot_front[at * backs : (at + 1) * backs, :]
            split[at, backs:sums] += front[at * BLOCK : (at + 1) * BLOCK, :]

    split_copies = []
    for step in range(1, n_col):
        copy = remote(
            split.at[col(step)], split_in.at[c], split_send.at[step], split_recv.at[c], col=col(step)
        )
        copy.start()
        split_copies.append(copy)
    z_step(4)
    z_step(5)

    for step in range(1, n_col):
        remote(
            split.at[0], split_in.at[col(step)], split_send.at[0], split_recv.at[col(step)], col=col(step)
        ).wait_recv()
    summed[...] = (split[c] + split_in[col(1)]) + (split_in[col(2)] + split_in[col(3)])
    summed_copies = []
    for step in range(1, n_gz):
        copy = remote(
            summed.at[pl.ds(0, sums), :], summed_in.at[g], summed_send.at[step], summed_recv.at[g], gz=gz(step)
        )
        copy.start()
        summed_copies.append(copy)

    def row_copy():
        return remote(summed.at[pl.ds(sums, BLOCK), :], row_in.at[g], row_send, row_recv.at[g], gz=r)

    @pl.when(g != r)
    def _():
        row_copy().start()

    z_step(6)
    z_step(7)
    for way in (1, -1):
        low_wait(way)
        low_pass(way).start()

    for step in range(1, n_gz):
        remote(
            summed.at[pl.ds(0, sums), :], summed_in.at[gz(step)], summed_send.at[0], summed_recv.at[gz(step)], gz=gz(step)
        ).wait_recv()
    total = summed[:sums, :]
    for step in range(1, n_gz):
        total += summed_in[gz(step)]
    panel[c] = total
    panel_copies = []
    for step in range(1, n_col):
        copy = remote(panel.at[c], panel.at[c], panel_send.at[step], panel_recv.at[c], col=col(step))
        copy.start()
        panel_copies.append(copy)

    def spread_copy(step):
        return remote(row_panel, row_panel, spread_send.at[step], spread_recv, row=row(step))

    @pl.when(g == r)
    def _():
        @pl.when(g != 0)
        def _():
            row_front_copy().wait_recv()

        total = summed[sums:, :] + row_front[...]
        for step in range(1, n_gz):
            remote(
                summed.at[pl.ds(sums, BLOCK), :], row_in.at[gz(step)], row_send, row_recv.at[gz(step)], gz=gz(step)
            ).wait_recv()
            total += row_in[gz(step)]
        row_panel[...] = total
        for step in range(1, n_row):
            spread_copy(step).start()

    z_step(8)
    z_step(9)
    for step in range(1, n_col):
        piece = panel.at[col(step)]
        remote(piece, piece, panel_send.at[0], panel_recv.at[col(step)], col=col(step)).wait_recv()
    pivot = jnp.concatenate([panel[at, :backs] for at in range(n_col)], axis=0)
    start_elimination(pivot, worked, product, lower_unit)
    pace = BLOCK // 8

    def factor_part(at):
        eliminate(at * pace, pace, worked, product, lower_unit, lower_inverse)

    def term_copy(j):
        return remote(terms.at[j], arrived.at[g], term_send.at[j], term_recv.at[g], gz=j)

    def term(distance):
        j = row(distance)
        for at in range(2):
            span = pl.ds(at * half, half)
            total = jnp.dot(lowers[0, span, :], gathered[j, 0], preferred_element_type=jnp.float32)
            for k_block in range(1, n_col):
                total += jnp.dot(
                    lowers[k_block, span, :], gathered[j, k_block], preferred_element_type=jnp.float32
                )
            terms[j, span, :] = total

        @pl.when(j != g)
        def _():
            term_copy(j).start()

    factor_part(0)
    z_step(10)
    z_step(11)
    factor_part(1)
    for way in (1, -1):
        low_far_wait(way)
    term(0)
    term(1)
    term(-1)
    factor_part(2)
    z_step(12)
    z_step(13)
    factor_part(3)
    term(2)
    term(-2)
    for at in range(4, 8):
        factor_part(at)

    for way in (1, -1):
        for place in range(n_col // 2):
            z_copy(way, last, place + (n_col // 2 if way > 0 else 0)).wait_recv()
    term(3)
    term(-3)

    upper_inverse = finish_elimination(worked, product, lower_unit)

    @pl.when(g != r)
    def _():
        spread_copy(1).wait_recv()

    upper = exact_dot(lower_inverse[...], row_panel[...])
    upper_panel[...] = upper
    for at in range(panels):
        span = pl.ds(at * BLOCK, BLOCK)
        lower = exact_dot(panel[at, backs:, :], upper_inverse)
        lower_panel[span, :] = lower
        trailing[span, :] = front[span, :] - exact_dot(lower, upper)

    for way in (1, -1):
        for place in range(n_col // 2):
            z_copy(way, last + 1, place + (0 if way > 0 else n_col // 2)).wait_recv()
    term(last + 1)

    for step in range(1, n_gz):
        block = arrived.at[gz(step)]
        remote(block, block, term_send.at[0], term_recv.at[gz(step)], gz=gz(step)).wait_recv()

    def add_up(at, carry):
        span = pl.ds(pl.multiple_of(at * BLOCK, BLOCK), BLOCK)
        total = terms[g, span, :]
        for step in range(1, n_gz):
            total += arrived[gz(step), span, :]
        trailing[span, :] -= total
        return carry

    lax.fori_loop(0, panels, add_up, 0)

    for copy in up_copies + z_copies + split_copies + summed_copies + panel_copies:
        copy.wait_send()
    for way in (1, -1):
        low_copy(way).wait_send()
        low_pass(way).wait_send()
    for step in range(1, n_gz):
        term_copy(gz(step)).wait_send()

    @pl.when(r < n_row // 2)
    def _():
        chain_sent(1)

    @pl.when((r == 0) | (r > n_row // 2 + 1))
    def _():
        chain_sent(-1)

    @pl.when((r == 0) & (g != 0))
    def _():
        row_front_copy().wait_send()

    @pl.when(g != r)
    def _():
        row_copy().wait_send()

    @pl.when(g == r)
    def _():
        for step in range(1, n_row):
            spread_copy(step).wait_send()


def shards(n_gz, n_row, n_col, subtree_lower, subtree_upper, touched, front):
    height, depth = subtree_lower.shape[1:]
    width = front.shape[3]
    bf16, f32 = jnp.bfloat16, jnp.float32
    dma = pltpu.SemaphoreType.DMA
    backs = BLOCK // n_col
    vmem = pl.BlockSpec(memory_space=pltpu.VMEM)
    lower_panel, upper_panel, trailing = pl.pallas_call(
        functools.partial(front_kernel, n_gz, n_row, n_col),
        out_shape=(
            jax.ShapeDtypeStruct((height, width), f32),
            jax.ShapeDtypeStruct((width, width), f32),
            jax.ShapeDtypeStruct((height, width), f32),
        ),
        in_specs=[vmem, vmem, pl.BlockSpec(memory_space=pltpu.SMEM), vmem],
        out_specs=(vmem, vmem, vmem),
        scratch_shapes=[
            pltpu.VMEM((n_col, height, depth), bf16),
            pltpu.VMEM((n_col, depth, BLOCK), bf16),
            pltpu.VMEM((n_row, n_col, depth, BLOCK), bf16),
            pltpu.VMEM((n_gz, height, BLOCK), f32),
            pltpu.VMEM((n_gz, height, BLOCK), f32),
            pltpu.VMEM((BLOCK, depth), bf16),
            pltpu.VMEM((depth, BLOCK), bf16),
            pltpu.VMEM((BLOCK, BLOCK), f32),
            pltpu.VMEM((BLOCK, BLOCK), f32),
            pltpu.VMEM((n_col, backs + 2 * BLOCK, BLOCK), f32),
            pltpu.VMEM((n_col, backs + 2 * BLOCK, BLOCK), f32),
            pltpu.VMEM((backs + 2 * BLOCK, BLOCK), f32),
            pltpu.VMEM((n_gz, backs + BLOCK, BLOCK), f32),
            pltpu.VMEM((n_gz, BLOCK, BLOCK), f32),
            pltpu.VMEM((n_col, backs + BLOCK, BLOCK), f32),
            pltpu.VMEM((BLOCK, BLOCK), f32),
            pltpu.VMEM((BLOCK, BLOCK), f32),
            pltpu.VMEM((BLOCK, BLOCK), f32),
            pltpu.VMEM((BLOCK, BLOCK), f32),
            pltpu.VMEM((BLOCK, BLOCK), f32),
            dma((n_col,)), dma((n_col,)),
            dma((4,)), dma((4,)),
            dma((2, n_row * n_col)), dma((n_row, n_col)),
            dma((n_gz,)), dma((n_gz,)),
            dma((2, 3)), dma((3,)),
            dma((2,)),
            dma((n_col,)), dma((n_col,)),
            dma((n_gz,)), dma((n_gz,)),
            dma, dma((n_gz,)),
            dma((n_col,)), dma((n_col,)),
            dma((n_row,)), dma,
        ],
        compiler_params=pltpu.CompilerParams(
            collective_id=0, has_side_effects=True, vmem_limit_bytes=48 * 1024 * 1024
        ),
    )(subtree_lower[0], subtree_upper[0], touched, front.reshape(height, width))
    return (
        lower_panel,
        upper_panel.reshape(width, 1, 1, width),
        trailing.reshape(height, 1, 1, width),
    )


def solution(mesh):
    placed = (
        P("gz", "row", "col"),
        P("gz", "col", "row"),
        P("gz", None),
        P("row", "gz", "col", None),
    )
    return jax.shard_map(
        functools.partial(shards, mesh.shape["gz"], mesh.shape["row"], mesh.shape["col"]),
        mesh=mesh,
        in_specs=placed,
        out_specs=(P("row", None), P(None, "gz", "col", None), P("row", "gz", "col", None)),
        check_vma=False,
    )
```

```python
import functools

import jax
import jax.numpy as jnp
from jax import lax
from jax.experimental import pallas as pl
from jax.experimental.pallas import tpu as pltpu
from jax.sharding import PartitionSpec as P

BLOCK = 128
MESH = pl.DeviceIdType.MESH
ORDER_OF_K = (0, 1, 3, 2)


def exact_dot(left, right):
    return jnp.dot(
        left, right, precision=lax.Precision.HIGHEST, preferred_element_type=jnp.float32
    )


def eliminate(first, count, worked, product, lower, lower_inverse):
    rows = lax.broadcasted_iota(jnp.int32, (BLOCK, BLOCK), 0)
    lanes = lax.broadcasted_iota(jnp.int32, (BLOCK, BLOCK), 1)

    def step(at, carry):
        dense = worked[...]
        pivot_row = worked[pl.ds(at, 1), :]
        product_row = product[pl.ds(at, 1), :]
        lower_inverse[pl.ds(at, 1), :] = product_row
        column = jnp.sum(jnp.where(lanes == at, dense, 0.0), axis=1, keepdims=True)
        pivot = jnp.sum(
            jnp.where(lanes[:1] == at, pivot_row, 0.0), axis=1, keepdims=True
        )
        scaled = jnp.where(rows == at, 0.0, column / pivot)
        worked[...] = dense - scaled * pivot_row
        product[...] = product[...] - scaled * product_row
        lower[...] = jnp.where((lanes == at) & (rows > at), scaled, lower[...])
        return carry

    lax.fori_loop(first, first + count, step, 0)


def start_elimination(pivot, worked, product, lower):
    rows = lax.broadcasted_iota(jnp.int32, (BLOCK, BLOCK), 0)
    lanes = lax.broadcasted_iota(jnp.int32, (BLOCK, BLOCK), 1)
    identity = jnp.where(rows == lanes, 1.0, 0.0)
    worked[...] = pivot
    product[...] = identity
    lower[...] = identity


def finish_elimination(worked, product, lower):
    rows = lax.broadcasted_iota(jnp.int32, (BLOCK, BLOCK), 0)
    lanes = lax.broadcasted_iota(jnp.int32, (BLOCK, BLOCK), 1)
    pivots = jnp.sum(jnp.where(rows == lanes, worked[...], 0.0), axis=1, keepdims=True)
    return exact_dot(product[...] / pivots, lower[...])


def remote(src, dst, send_sem, recv_sem, **where):
    return pltpu.make_async_remote_copy(
        src_ref=src,
        dst_ref=dst,
        send_sem=send_sem,
        recv_sem=recv_sem,
        device_id=where,
        device_id_type=MESH,
    )


def front_kernel(
    n_gz, n_row, n_col,
    lower_hbm, upper_hbm, touched_hbm, front_hbm,
    lower_panel, upper_panel, trailing,
    lower_in, upper_in, touched, front,
    lowers, uppers, gathered, terms, pair_out, pair_in, arrived,
    first_rows, first_columns, row_front,
    pivot_split, pivot_split_in, pivot_sum, pivot_sum_in, pivot,
    split, split_in, summed, summed_in, row_in, panel, row_panel,
    worked, product, lower_unit, lower_inverse,
    in_sem, up_send, up_recv, low_send, low_recv, z_send, z_recv, term_send, term_recv,
    pair_send, pair_recv, chain_send, chain_recv, row_front_sem,
    pivot_split_send, pivot_split_recv, pivot_sum_send, pivot_sum_recv,
    pivot_row_send, pivot_row_recv, pivot_col_send, pivot_col_recv,
    split_send, split_recv, summed_send, summed_recv,
    row_send, row_recv, panel_send, panel_recv, spread_send, spread_recv,
):
    g, r, c = lax.axis_index("gz"), lax.axis_index("row"), lax.axis_index("col")
    height = lower_in.shape[0]
    panels = height // BLOCK
    half = height // 2
    backs = BLOCK // n_col
    x, core = g // 2, lax.rem(g, 2)
    sibling = g + 1 - 2 * core
    sends = []

    def gz(step):
        return lax.rem(g + step, n_gz)

    def row(step):
        return lax.rem(r + n_row + step, n_row)

    def col(step):
        return lax.rem(c + n_col + step, n_col)

    def start(copy):
        copy.start()
        sends.append(copy)

    inputs = [
        pltpu.make_async_copy(upper_hbm, upper_in, in_sem.at[0]),
        pltpu.make_async_copy(touched_hbm, touched, in_sem.at[1]),
        pltpu.make_async_copy(lower_hbm, lower_in, in_sem.at[2]),
        pltpu.make_async_copy(front_hbm, front, in_sem.at[3]),
    ]
    for copy in inputs:
        copy.start()

    barrier = pltpu.get_barrier_semaphore()
    for step in range(1, n_gz):
        pl.semaphore_signal(barrier, inc=1, device_id={"gz": gz(step)}, device_id_type=MESH)
    for step in range(1, n_row):
        pl.semaphore_signal(barrier, inc=1, device_id={"row": row(step)}, device_id_type=MESH)
    for step in range(1, n_col):
        pl.semaphore_signal(barrier, inc=1, device_id={"col": col(step)}, device_id_type=MESH)

    for copy in inputs:
        copy.wait()
    for at in range(panels):
        mark = touched[0, r * panels + at].astype(jnp.float32)
        span = pl.ds(at * BLOCK, BLOCK)
        uppers[at] = (upper_in[:, span].astype(jnp.float32) * mark).astype(jnp.bfloat16)
        lowers[c, span, :] = (lower_in[span, :].astype(jnp.float32) * mark).astype(jnp.bfloat16)
    gathered[r, c] = uppers[c]
    corner = (g == 0) & (c == 0)

    @pl.when(r == 0)
    def _():
        first_rows[...] = lowers[c, :BLOCK, :]
        first_columns[...] = uppers[0]
        part = -jnp.dot(lowers[c, :BLOCK, :], uppers[0], preferred_element_type=jnp.float32)
        for at in range(n_col):
            pivot_split[at] = part[at * backs : (at + 1) * backs]

    @pl.when((r == 0) & (g == 0))
    def _():
        row_front[...] = front[:BLOCK, :]

    @pl.when((r == 0) & corner)
    def _():
        for at in range(n_col):
            pivot_split[at] += front[at * backs : (at + 1) * backs, :]

    pl.semaphore_wait(barrier, n_gz + n_row + n_col - 3)

    def pivot_split_copy(step):
        return remote(
            pivot_split.at[col(step)], pivot_split_in.at[c],
            pivot_split_send.at[step], pivot_split_recv.at[c], col=col(step),
        )

    def pivot_sum_copy(step):
        return remote(
            pivot_sum, pivot_sum_in.at[g], pivot_sum_send.at[step], pivot_sum_recv.at[g], gz=gz(step)
        )

    def pivot_row_copy(step):
        piece = pivot.at[c]
        return remote(piece, piece, pivot_row_send.at[step], pivot_row_recv, row=row(step))

    def pivot_over_col():
        @pl.when(r == 0)
        def _():
            for step in range(1, n_col):
                remote(
                    pivot_split.at[0], pivot_split_in.at[col(step)],
                    pivot_split_send.at[0], pivot_split_recv.at[col(step)], col=col(step),
                ).wait_recv()
            total = pivot_split[c]
            for step in range(1, n_col):
                total += pivot_split_in[col(step)]
            pivot_sum[...] = total
            for step in range(1, n_gz):
                pivot_sum_copy(step).start()

    def pivot_over_gz():
        @pl.when(r == 0)
        def _():
            for step in range(1, n_gz):
                remote(
                    pivot_sum, pivot_sum_in.at[gz(step)],
                    pivot_sum_send.at[0], pivot_sum_recv.at[gz(step)], gz=gz(step),
                ).wait_recv()
            total = pivot_sum[...]
            for step in range(1, n_gz):
                total += pivot_sum_in[gz(step)]
            pivot[c] = total
            for step in range(1, n_row):
                pivot_row_copy(step).start()

    def pivot_out():
        @pl.when(r != 0)
        def _():
            pivot_row_copy(1).wait_recv()

        for step in range(1, n_col):
            piece = pivot.at[c]
            start(remote(piece, piece, pivot_col_send.at[step], pivot_col_recv.at[c], col=col(step)))

    def pivot_done():
        for step in range(1, n_col):
            piece = pivot.at[col(step)]
            remote(
                piece, piece, pivot_col_send.at[0], pivot_col_recv.at[col(step)], col=col(step)
            ).wait_recv()
        whole = jnp.concatenate([pivot[at] for at in range(n_col)], axis=0)
        start_elimination(whole, worked, product, lower_unit)

    def chain(way, at):
        slot = 0 if way > 0 else 1
        buffer = (first_columns, first_rows)[at]
        return remote(buffer, buffer, chain_send.at[slot, at], chain_recv.at[at], row=row(way))

    def chain_hop(hop):
        def pass_on(way):
            for at in range(2):
                chain(1, at).wait_recv()
                if way:
                    chain(way, at).start()

        @pl.when(r == hop)
        def _():
            pass_on(1 if hop < n_row // 2 else 0)

        if hop < n_row // 2:
            @pl.when(r == n_row - hop)
            def _():
                pass_on(-1 if hop < n_row // 2 - 1 else 0)

    def row_front_copy():
        return remote(
            front.at[pl.ds(0, BLOCK), :], row_front, row_front_sem.at[0], row_front_sem.at[1], row=g
        )

    def up_arrive(step):
        remote(
            uppers.at[0], gathered.at[r, col(step)], up_send.at[0], up_recv.at[col(step)], col=col(step)
        ).wait_recv()

    def z_copy(way, distance, place):
        source = row(-way * distance)
        k_block = col(ORDER_OF_K[place])
        piece = gathered.at[source, k_block]
        slot = 0 if way > 0 else 1
        at = distance * n_col + place
        return remote(piece, piece, z_send.at[slot, at], z_recv.at[source, k_block], row=row(way))

    last = n_row // 2 - 1
    z_order = [(distance, place) for distance in range(last) for place in range(n_col)]
    z_order += [(last, place) for place in range(n_col // 2)]

    def z_step(at):
        distance, place = z_order[at]
        if distance == 0 and place > 0:
            up_arrive(ORDER_OF_K[place])
        for way in (1, -1):
            used = place
            if distance == last and way < 0:
                used = place + n_col // 2
            copy = z_copy(way, distance, used)
            if distance > 0:
                copy.wait_recv()
            start(copy)

    def low_copy(way):
        slot = 0 if way > 0 else 1
        return remote(
            lowers.at[c], lowers.at[c], low_send.at[slot], low_recv.at[slot], col=col(way)
        )

    def low_pass(way):
        slot = 0 if way > 0 else 1
        block = lowers.at[col(-way)]
        remote(block, block, low_send.at[slot], low_recv.at[slot], col=col(way)).wait_recv()
        piece = lowers.at[col(-way), pl.ds(slot * half, half), :]
        start(remote(piece, piece, low_send.at[2 + slot], low_recv.at[2 + slot], col=col(way)))

    def low_far_wait(way):
        slot = 0 if way > 0 else 1
        piece = lowers.at[col(2), pl.ds(slot * half, half), :]
        remote(piece, piece, low_send.at[2 + slot], low_recv.at[2 + slot], col=col(way)).wait_recv()

    def panel_products():
        column = first_columns[...]
        for at in range(n_col):
            split[at, :BLOCK] = -jnp.dot(
                lowers[c, at * BLOCK : (at + 1) * BLOCK, :], column, preferred_element_type=jnp.float32
            )
            split[at, BLOCK:] = -jnp.dot(
                first_rows[...], uppers[at], preferred_element_type=jnp.float32
            )

        @pl.when(corner)
        def _():
            for at in range(n_col):
                split[at, :BLOCK] += front[at * BLOCK : (at + 1) * BLOCK, :]

        for step in range(1, n_col):
            start(
                remote(
                    split.at[col(step)], split_in.at[c],
                    split_send.at[step], split_recv.at[c], col=col(step),
                )
            )

    def row_copy():
        return remote(summed.at[pl.ds(BLOCK, BLOCK), :], row_in.at[g], row_send, row_recv.at[g], gz=r)

    def panel_over_col():
        for step in range(1, n_col):
            remote(
                split.at[0], split_in.at[col(step)],
                split_send.at[0], split_recv.at[col(step)], col=col(step),
            ).wait_recv()
        total = split[c]
        for step in range(1, n_col):
            total += split_in[col(step)]
        summed[...] = total

        @pl.when(g != r)
        def _():
            row_copy().start()

        for step in range(1, n_gz):
            start(
                remote(
                    summed.at[pl.ds(0, BLOCK), :], summed_in.at[g],
                    summed_send.at[step], summed_recv.at[g], gz=gz(step),
                )
            )

    def spread_copy(step):
        return remote(row_panel, row_panel, spread_send.at[step], spread_recv, row=row(step))

    def panel_over_gz():
        @pl.when(g == r)
        def _():
            @pl.when(g != 0)
            def _():
                row_front_copy().wait_recv()

            total = summed[BLOCK:, :] + row_front[...]
            for step in range(1, n_gz):
                remote(
                    summed.at[pl.ds(BLOCK, BLOCK), :], row_in.at[gz(step)],
                    row_send, row_recv.at[gz(step)], gz=gz(step),
                ).wait_recv()
                total += row_in[gz(step)]
            row_panel[...] = total
            for step in range(1, n_row):
                spread_copy(step).start()

        total = summed[:BLOCK, :]
        for step in range(1, n_gz):
            remote(
                summed.at[pl.ds(0, BLOCK), :], summed_in.at[gz(step)],
                summed_send.at[0], summed_recv.at[gz(step)], gz=gz(step),
            ).wait_recv()
            total += summed_in[gz(step)]
        panel[c] = total
        for step in range(1, n_col):
            start(
                remote(panel.at[c], panel.at[c], panel_send.at[step], panel_recv.at[c], col=col(step))
            )

    def panel_done():
        for step in range(1, n_col):
            piece = panel.at[col(step)]
            remote(piece, piece, panel_send.at[0], panel_recv.at[col(step)], col=col(step)).wait_recv()

        @pl.when(g != r)
        def _():
            spread_copy(1).wait_recv()

    done = [0]

    def factor_part(count):
        eliminate(done[0], count, worked, product, lower_unit, lower_inverse)
        done[0] += count

    def term_copy(j):
        span = pl.ds(pl.multiple_of(core * half, half), half)
        return remote(terms.at[j], arrived.at[x, span, :], term_send.at[j], term_recv.at[g], gz=j)

    def layer_rows(j, which):
        span = pl.ds(pl.multiple_of(which * half, half), half)
        total = jnp.dot(lowers[0, span, :], gathered[j, 0], preferred_element_type=jnp.float32)
        for k_block in range(1, n_col):
            total += jnp.dot(
                lowers[k_block, span, :], gathered[j, k_block], preferred_element_type=jnp.float32
            )
        return total

    def pair_copy(j):
        return remote(pair_out.at[j], pair_in.at[j], pair_send.at[j], pair_recv.at[j], gz=sibling)

    def term(distance):
        j = row(distance)
        pair_out[j] = layer_rows(j, 1 - core)
        start(pair_copy(j))
        terms[j] = layer_rows(j, core)

    def term_out(distance):
        j = row(distance)
        pair_copy(j).wait_recv()
        terms[j] += pair_in[j]

        @pl.when(j != g)
        def _():
            term_copy(j).start()

        @pl.when(j == g)
        def _():
            arrived[x, pl.ds(pl.multiple_of(core * half, half), half), :] = terms[j]

    @pl.when(r == 0)
    def _():
        for step in range(1, n_col):
            pivot_split_copy(step).start()
        for at in range(2):
            chain(1, at).start()
            chain(-1, at).start()

    for slot, step in enumerate(ORDER_OF_K[1:]):
        start(
            remote(
                uppers.at[col(step)], gathered.at[r, c], up_send.at[slot], up_recv.at[c], col=col(step)
            )
        )
    z_step(0)
    for way in (1, -1):
        start(low_copy(way))

    @pl.when((r == 0) & (g != 0))
    def _():
        row_front_copy().start()

    pivot_over_col()
    z_step(1)
    chain_hop(1)
    z_step(2)
    pivot_over_gz()
    z_step(3)
    chain_hop(2)
    z_step(4)
    pivot_out()
    z_step(5)
    chain_hop(3)
    pivot_done()
    factor_part(8)
    z_step(6)
    factor_part(8)
    chain_hop(4)
    panel_products()
    z_step(7)
    for way in (1, -1):
        low_pass(way)
    factor_part(16)
    z_step(8)
    panel_over_col()
    factor_part(16)
    z_step(9)
    factor_part(16)
    panel_over_gz()
    z_step(10)
    for way in (1, -1):
        low_far_wait(way)
    term(0)
    term(1)
    term_out(0)
    factor_part(16)
    z_step(11)
    term(-1)
    term_out(1)
    factor_part(16)
    z_step(12)
    term_out(-1)
    term(2)
    factor_part(16)
    z_step(13)
    term(-2)
    term_out(2)
    factor_part(16)
    term_out(-2)
    upper_inverse = finish_elimination(worked, product, lower_unit)

    for way in (1, -1):
        for place in range(n_col // 2):
            z_copy(way, last, place + (n_col // 2 if way > 0 else 0)).wait_recv()
    term(3)
    term(-3)
    term_out(3)
    term_out(-3)

    panel_done()
    upper = exact_dot(lower_inverse[...], row_panel[...])
    upper_panel[...] = upper
    for at in range(panels):
        span = pl.ds(at * BLOCK, BLOCK)
        lower = exact_dot(panel[at], upper_inverse)
        lower_panel[span, :] = lower
        trailing[span, :] = front[span, :] - exact_dot(lower, upper)

    for way in (1, -1):
        for place in range(n_col // 2):
            z_copy(way, last + 1, place + (0 if way > 0 else n_col // 2)).wait_recv()
    term(last + 1)
    term_out(last + 1)

    for step in range(1, n_gz):
        other = gz(step)
        span = pl.ds(pl.multiple_of(lax.rem(other, 2) * half, half), half)
        block = arrived.at[other // 2, span, :]
        remote(block, block, term_send.at[0], term_recv.at[other], gz=other).wait_recv()

    def add_up(at, carry):
        span = pl.ds(pl.multiple_of(at * BLOCK, BLOCK), BLOCK)
        total = arrived[0, span, :]
        for chip in range(1, n_gz // 2):
            total += arrived[chip, span, :]
        trailing[span, :] -= total
        return carry

    lax.fori_loop(0, panels, add_up, 0)

    for copy in sends:
        copy.wait_send()
    for step in range(1, n_gz):
        term_copy(gz(step)).wait_send()

    @pl.when(r < n_row // 2)
    def _():
        for at in range(2):
            chain(1, at).wait_send()

    @pl.when((r == 0) | (r > n_row // 2 + 1))
    def _():
        for at in range(2):
            chain(-1, at).wait_send()

    @pl.when(r == 0)
    def _():
        for step in range(1, n_col):
            pivot_split_copy(step).wait_send()
        for step in range(1, n_gz):
            pivot_sum_copy(step).wait_send()
        for step in range(1, n_row):
            pivot_row_copy(step).wait_send()

    @pl.when((r == 0) & (g != 0))
    def _():
        row_front_copy().wait_send()

    @pl.when(g != r)
    def _():
        row_copy().wait_send()

    @pl.when(g == r)
    def _():
        for step in range(1, n_row):
            spread_copy(step).wait_send()


def shards(n_gz, n_row, n_col, subtree_lower, subtree_upper, touched, front):
    height, depth = subtree_lower.shape[1:]
    width = front.shape[3]
    half = height // 2
    bf16, f32 = jnp.bfloat16, jnp.float32
    dma = pltpu.SemaphoreType.DMA
    backs = BLOCK // n_col
    vmem = pl.BlockSpec(memory_space=pltpu.VMEM)
    anywhere = pl.BlockSpec(memory_space=pltpu.HBM)
    lower_panel, upper_panel, trailing = pl.pallas_call(
        functools.partial(front_kernel, n_gz, n_row, n_col),
        out_shape=(
            jax.ShapeDtypeStruct((height, width), f32),
            jax.ShapeDtypeStruct((width, width), f32),
            jax.ShapeDtypeStruct((height, width), f32),
        ),
        in_specs=[anywhere] * 4,
        out_specs=(vmem, vmem, vmem),
        scratch_shapes=[
            pltpu.VMEM((height, depth), bf16),
            pltpu.VMEM((depth, height), bf16),
            pltpu.SMEM(touched.shape, jnp.int32),
            pltpu.VMEM((height, width), f32),
            pltpu.VMEM((n_col, height, depth), bf16),
            pltpu.VMEM((n_col, depth, BLOCK), bf16),
            pltpu.VMEM((n_row, n_col, depth, BLOCK), bf16),
            pltpu.VMEM((n_gz, half, BLOCK), f32),
            pltpu.VMEM((n_gz, half, BLOCK), f32),
            pltpu.VMEM((n_gz, half, BLOCK), f32),
            pltpu.VMEM((n_gz // 2, height, BLOCK), f32),
            pltpu.VMEM((BLOCK, depth), bf16),
            pltpu.VMEM((depth, BLOCK), bf16),
            pltpu.VMEM((BLOCK, BLOCK), f32),
            pltpu.VMEM((n_col, backs, BLOCK), f32),
            pltpu.VMEM((n_col, backs, BLOCK), f32),
            pltpu.VMEM((backs, BLOCK), f32),
            pltpu.VMEM((n_gz, backs, BLOCK), f32),
            pltpu.VMEM((n_col, backs, BLOCK), f32),
            pltpu.VMEM((n_col, 2 * BLOCK, BLOCK), f32),
            pltpu.VMEM((n_col, 2 * BLOCK, BLOCK), f32),
            pltpu.VMEM((2 * BLOCK, BLOCK), f32),
            pltpu.VMEM((n_gz, BLOCK, BLOCK), f32),
            pltpu.VMEM((n_gz, BLOCK, BLOCK), f32),
            pltpu.VMEM((n_col, BLOCK, BLOCK), f32),
            pltpu.VMEM((BLOCK, BLOCK), f32),
            pltpu.VMEM((BLOCK, BLOCK), f32),
            pltpu.VMEM((BLOCK, BLOCK), f32),
            pltpu.VMEM((BLOCK, BLOCK), f32),
            pltpu.VMEM((BLOCK, BLOCK), f32),
            dma((4,)),
            dma((n_col,)), dma((n_col,)),
            dma((4,)), dma((4,)),
            dma((2, n_row * n_col)), dma((n_row, n_col)),
            dma((n_gz,)), dma((n_gz,)),
            dma((n_gz,)), dma((n_gz,)),
            dma((2, 2)), dma((2,)),
            dma((2,)),
            dma((n_col,)), dma((n_col,)),
            dma((n_gz,)), dma((n_gz,)),
            dma((n_row,)), dma,
            dma((n_col,)), dma((n_col,)),
            dma((n_col,)), dma((n_col,)),
            dma((n_gz,)), dma((n_gz,)),
            dma, dma((n_gz,)),
            dma((n_col,)), dma((n_col,)),
            dma((n_row,)), dma,
        ],
        compiler_params=pltpu.CompilerParams(
            collective_id=0, has_side_effects=True, vmem_limit_bytes=48 * 1024 * 1024
        ),
    )(subtree_lower[0], subtree_upper[0], touched, front.reshape(height, width))
    return (
        lower_panel,
        upper_panel.reshape(width, 1, 1, width),
        trailing.reshape(height, 1, 1, width),
    )


def solution(mesh):
    placed = (
        P("gz", "row", "col"),
        P("gz", "col", "row"),
        P("gz", None),
        P("row", "gz", "col", None),
    )
    return jax.shard_map(
        functools.partial(shards, mesh.shape["gz"], mesh.shape["row"], mesh.shape["col"]),
        mesh=mesh,
        in_specs=placed,
        out_specs=(P("row", None), P(None, "gz", "col", None), P("row", "gz", "col", None)),
        check_vma=False,
    )
```

```python
import functools

import jax
import jax.numpy as jnp
from jax import lax
from jax.experimental import pallas as pl
from jax.experimental.pallas import tpu as pltpu
from jax.sharding import PartitionSpec as P

BLOCK = 128
MESH = pl.DeviceIdType.MESH
ORDER_OF_K = (0, 1, 3, 2)
NATURAL = [(away, place) for away in range(3) for place in range(4)] + [(3, 0), (3, 1)]
OWN, NEXT, FAR = NATURAL[0:4], NATURAL[4:8], NATURAL[8:12]
RING = {
    1: OWN[:2] + NEXT + OWN[2:] + FAR + [(3, 0), (3, 1)],
    2: OWN + FAR + NEXT + [(3, 0), (3, 1)],
    3: OWN + NEXT[:2] + [(3, 0), (3, 1)] + NEXT[2:] + FAR,
}
RING_BACK = {1: RING[1], 2: RING[2], 3: OWN + NEXT + [(3, 0), (3, 1)] + FAR}


def exact_dot(left, right):
    return jnp.dot(
        left, right, precision=lax.Precision.HIGHEST, preferred_element_type=jnp.float32
    )


def eliminate(first, count, worked, product, upper, lower_inverse):
    rows = lax.broadcasted_iota(jnp.int32, (BLOCK, BLOCK), 0)
    lanes = lax.broadcasted_iota(jnp.int32, (BLOCK, BLOCK), 1)

    def step(at, carry):
        dense = worked[...]
        pivot_row = worked[pl.ds(at, 1), :]
        product_row = product[pl.ds(at, 1), :]
        lower_inverse[pl.ds(at, 1), :] = product_row
        column = jnp.sum(jnp.where(lanes == at, dense, 0.0), axis=1, keepdims=True)
        pivot = jnp.sum(
            jnp.where(lanes[:1] == at, pivot_row, 0.0), axis=1, keepdims=True
        )
        scaled = jnp.where(rows == at, 0.0, column / pivot)
        worked[...] = dense - scaled * pivot_row
        product[...] = product[...] - scaled * product_row
        upper[...] = jnp.where((lanes == at) & (rows < at), -scaled, upper[...])
        return carry

    lax.fori_loop(first, first + count, step, 0)


def start_elimination(pivot, worked, product, upper):
    rows = lax.broadcasted_iota(jnp.int32, (BLOCK, BLOCK), 0)
    lanes = lax.broadcasted_iota(jnp.int32, (BLOCK, BLOCK), 1)
    identity = jnp.where(rows == lanes, 1.0, 0.0)
    worked[...] = pivot
    product[...] = identity
    upper[...] = identity


def finish_elimination(worked, upper):
    rows = lax.broadcasted_iota(jnp.int32, (BLOCK, BLOCK), 0)
    lanes = lax.broadcasted_iota(jnp.int32, (BLOCK, BLOCK), 1)
    pivots = jnp.sum(jnp.where(rows == lanes, worked[...], 0.0), axis=1, keepdims=True)
    return upper[...] / pivots


def remote(src, dst, send_sem, recv_sem, **where):
    return pltpu.make_async_remote_copy(
        src_ref=src,
        dst_ref=dst,
        send_sem=send_sem,
        recv_sem=recv_sem,
        device_id=where,
        device_id_type=MESH,
    )


def front_kernel(
    n_gz, n_row, n_col,
    lower_hbm, upper_hbm, touched_hbm, front_hbm,
    lower_panel, upper_panel, trailing,
    lower_in, upper_in, touched, front,
    lowers, uppers, gathered, terms, pair_out, pair_in, arrived,
    first_rows, row_front,
    pivot_split, pivot_split_in, pivot_sum, pivot_sum_in, pivot,
    split, split_in, summed, row_in, row_panel, column_part, column_in, panel,
    worked, product, upper_unit, lower_inverse,
    in_sem, up_send, up_recv, low_send, low_recv, z_send, z_recv, term_send, term_recv,
    pair_send, pair_recv, chain_send, chain_recv, row_front_sem,
    pivot_split_send, pivot_split_recv, pivot_sum_send, pivot_sum_recv,
    pivot_row_send, pivot_row_recv, pivot_col_send, pivot_col_recv,
    split_send, split_recv, row_send, row_recv, spread_send, spread_recv,
    column_send, column_recv, hand_send, hand_recv, panel_send, panel_recv,
):
    g, r, c = lax.axis_index("gz"), lax.axis_index("row"), lax.axis_index("col")
    height = lower_in.shape[0]
    panels = height // BLOCK
    half = height // 2
    backs = BLOCK // n_col
    x, core = g // 2, lax.rem(g, 2)
    sibling = g + 1 - 2 * core
    sends = []

    def gz(step):
        return lax.rem(g + step, n_gz)

    def row(step):
        return lax.rem(r + n_row + step, n_row)

    def col(step):
        return lax.rem(c + n_col + step, n_col)

    def start(copy):
        copy.start()
        sends.append(copy)

    inputs = [
        pltpu.make_async_copy(upper_hbm, upper_in, in_sem.at[0]),
        pltpu.make_async_copy(touched_hbm, touched, in_sem.at[1]),
        pltpu.make_async_copy(lower_hbm, lower_in, in_sem.at[2]),
        pltpu.make_async_copy(front_hbm, front, in_sem.at[3]),
    ]
    for copy in inputs:
        copy.start()

    barrier = pltpu.get_barrier_semaphore()
    for step in range(1, n_gz):
        pl.semaphore_signal(barrier, inc=1, device_id={"gz": gz(step)}, device_id_type=MESH)
    for step in range(1, n_row):
        pl.semaphore_signal(barrier, inc=1, device_id={"row": row(step)}, device_id_type=MESH)
    for step in range(1, n_col):
        pl.semaphore_signal(barrier, inc=1, device_id={"col": col(step)}, device_id_type=MESH)

    for copy in inputs:
        copy.wait()
    for at in range(panels):
        mark = touched[0, r * panels + at].astype(jnp.float32)
        span = pl.ds(at * BLOCK, BLOCK)
        uppers[at] = (upper_in[:, span].astype(jnp.float32) * mark).astype(jnp.bfloat16)
        lowers[c, span, :] = (lower_in[span, :].astype(jnp.float32) * mark).astype(jnp.bfloat16)
    gathered[r, c] = uppers[c]
    corner = (g == 0) & (c == 0)
    strip = height // n_gz

    @pl.when(r == 0)
    def _():
        first_rows[...] = lowers[c, :BLOCK, :]
        part = -jnp.dot(lowers[c, :BLOCK, :], uppers[0], preferred_element_type=jnp.float32)
        for at in range(n_col):
            pivot_split[at] = part[at * backs : (at + 1) * backs]

    @pl.when((r == 0) & (g == 0))
    def _():
        row_front[...] = front[:BLOCK, :]

    @pl.when((r == 0) & corner)
    def _():
        for at in range(n_col):
            pivot_split[at] += front[at * backs : (at + 1) * backs, :]

    pl.semaphore_wait(barrier, n_gz + n_row + n_col - 3)

    def pivot_split_copy(step):
        return remote(
            pivot_split.at[col(step)], pivot_split_in.at[c],
            pivot_split_send.at[step], pivot_split_recv.at[c], col=col(step),
        )

    def pivot_sum_copy(step):
        return remote(
            pivot_sum, pivot_sum_in.at[g], pivot_sum_send.at[step], pivot_sum_recv.at[g], gz=gz(step)
        )

    def pivot_row_copy(step):
        piece = pivot.at[c]
        return remote(piece, piece, pivot_row_send.at[step], pivot_row_recv, row=row(step))

    def pivot_over_col():
        @pl.when(r == 0)
        def _():
            for step in range(1, n_col):
                remote(
                    pivot_split.at[0], pivot_split_in.at[col(step)],
                    pivot_split_send.at[0], pivot_split_recv.at[col(step)], col=col(step),
                ).wait_recv()
            total = pivot_split[c]
            for step in range(1, n_col):
                total += pivot_split_in[col(step)]
            pivot_sum[...] = total
            for step in range(1, n_gz):
                pivot_sum_copy(step).start()

    def pivot_over_gz():
        @pl.when(r == 0)
        def _():
            for step in range(1, n_gz):
                remote(
                    pivot_sum, pivot_sum_in.at[gz(step)],
                    pivot_sum_send.at[0], pivot_sum_recv.at[gz(step)], gz=gz(step),
                ).wait_recv()
            total = pivot_sum[...]
            for step in range(1, n_gz):
                total += pivot_sum_in[gz(step)]
            pivot[c] = total
            for step in range(1, n_row):
                pivot_row_copy(step).start()

    def pivot_out():
        @pl.when(r != 0)
        def _():
            pivot_row_copy(1).wait_recv()

        for step in range(1, n_col):
            piece = pivot.at[c]
            start(remote(piece, piece, pivot_col_send.at[step], pivot_col_recv.at[c], col=col(step)))

    def pivot_done():
        for step in range(1, n_col):
            piece = pivot.at[col(step)]
            remote(
                piece, piece, pivot_col_send.at[0], pivot_col_recv.at[col(step)], col=col(step)
            ).wait_recv()
        whole = jnp.concatenate([pivot[at] for at in range(n_col)], axis=0)
        start_elimination(whole, worked, product, upper_unit)

    def chain(way, at):
        slot = 0 if way > 0 else 1
        piece = first_rows.at[pl.ds(at * (BLOCK // 2), BLOCK // 2), :]
        return remote(piece, piece, chain_send.at[slot, at], chain_recv.at[at], row=row(way))

    def chain_hop(hop):
        def pass_on(way):
            for at in range(2):
                chain(1, at).wait_recv()
                if way:
                    chain(way, at).start()

        @pl.when(r == hop)
        def _():
            pass_on(1 if hop < n_row // 2 else 0)

        if hop < n_row // 2:
            @pl.when(r == n_row - hop)
            def _():
                pass_on(-1 if hop < n_row // 2 - 1 else 0)

    def row_front_copy():
        return remote(
            front.at[pl.ds(0, BLOCK), :], row_front, row_front_sem.at[0], row_front_sem.at[1], row=g
        )

    def up_arrive(step):
        remote(
            uppers.at[0], gathered.at[r, col(step)], up_send.at[0], up_recv.at[col(step)], col=col(step)
        ).wait_recv()

    def z_wait(source, place):
        k_block = col(ORDER_OF_K[place])
        piece = gathered.at[source, k_block]
        remote(piece, piece, z_send.at[0, 0], z_recv.at[source, k_block], row=row(1)).wait_recv()

    last = n_row // 2 - 1

    def ring_entry(way, at):
        def entry(order):
            away, place = order[at]
            if away == last and way < 0:
                place += n_col // 2
            return away, ORDER_OF_K[place]

        from_first = r if way > 0 else lax.rem(n_row - r, n_row)
        away, offset = entry(NATURAL)
        if all(entry(order) == (away, offset) for order in (RING if way > 0 else RING_BACK).values()):
            return away, offset
        for distance, order in (RING if way > 0 else RING_BACK).items():
            here = from_first == distance
            away = jnp.where(here, entry(order)[0], away)
            offset = jnp.where(here, entry(order)[1], offset)
        return away, offset

    def z_step(at):
        if 0 < at < n_col:
            up_arrive(ORDER_OF_K[at])
        for way in (1, -1):
            away, offset = ring_entry(way, at)
            source, k_block = row(-way * away), col(offset)
            piece = gathered.at[source, k_block]
            slot = 0 if way > 0 else 1
            copy = remote(piece, piece, z_send.at[slot, at], z_recv.at[source, k_block], row=row(way))
            if not isinstance(away, int):
                pl.when(away > 0)(copy.wait_recv)
            elif away > 0:
                copy.wait_recv()
            start(copy)

    def far_wait(distance, way, places):
        source = row(-way * distance)

        @pl.when(source != 0)
        def _():
            for place in places:
                z_wait(source, place)

    def low_copy(way):
        slot = 0 if way > 0 else 1
        return remote(
            lowers.at[c], lowers.at[c], low_send.at[slot], low_recv.at[slot], col=col(way)
        )

    def low_pass(way):
        slot = 0 if way > 0 else 1
        block = lowers.at[col(-way)]
        remote(block, block, low_send.at[slot], low_recv.at[slot], col=col(way)).wait_recv()
        piece = lowers.at[col(-way), pl.ds(slot * half, half), :]
        start(remote(piece, piece, low_send.at[2 + slot], low_recv.at[2 + slot], col=col(way)))

    def low_far_wait(way):
        slot = 0 if way > 0 else 1
        piece = lowers.at[col(2), pl.ds(slot * half, half), :]
        remote(piece, piece, low_send.at[2 + slot], low_recv.at[2 + slot], col=col(way)).wait_recv()

    def row_products():
        for at in range(n_col):
            split[at] = -jnp.dot(first_rows[...], uppers[at], preferred_element_type=jnp.float32)
        for step in range(1, n_col):
            start(
                remote(
                    split.at[col(step)], split_in.at[c],
                    split_send.at[step], split_recv.at[c], col=col(step),
                )
            )

    def row_copy():
        return remote(summed, row_in.at[g], row_send, row_recv.at[g], gz=r)

    def row_over_col():
        for step in range(1, n_col):
            remote(
                split.at[0], split_in.at[col(step)],
                split_send.at[0], split_recv.at[col(step)], col=col(step),
            ).wait_recv()
        total = split[c]
        for step in range(1, n_col):
            total += split_in[col(step)]
        summed[...] = total

        @pl.when(g != r)
        def _():
            row_copy().start()

    def spread_copy(step):
        return remote(row_panel, row_panel, spread_send.at[step], spread_recv, row=row(step))

    def row_over_gz():
        @pl.when(g == r)
        def _():
            @pl.when(g != 0)
            def _():
                row_front_copy().wait_recv()

            total = summed[...] + row_front[...]
            for step in range(1, n_gz):
                remote(
                    summed, row_in.at[gz(step)], row_send, row_recv.at[gz(step)], gz=gz(step)
                ).wait_recv()
                total += row_in[gz(step)]
            row_panel[...] = total
            for step in range(1, n_row):
                spread_copy(step).start()

    def strip_of(at):
        return pl.ds(pl.multiple_of(at * strip, strip), strip)

    def column_copy(step):
        return remote(
            column_part.at[strip_of(gz(step)), :], column_in.at[g],
            column_send.at[step], column_recv.at[g], gz=gz(step),
        )

    def hand_copy(step):
        piece = panel.at[strip_of(g), :]
        return remote(piece, piece, hand_send.at[step], hand_recv, col=col(step))

    def column_product():
        far = n_row // 2
        for plane, places in ((far - 1, (2, 3)), (far, (0, 1, 2, 3)), (far + 1, (0, 1))):
            @pl.when(r == plane)
            def _():
                for place in places:
                    z_wait(0, place)

        @pl.when(c == 0)
        def _():
            for which in range(2):
                column_part[which * half : (which + 1) * half, :] = -layer_rows(0, which)

            @pl.when(g == 0)
            def _():
                column_part[...] += front[...]

            for step in range(1, n_gz):
                column_copy(step).start()

    def column_over_gz():
        @pl.when(c == 0)
        def _():
            total = column_part[strip_of(g), :]
            for step in range(1, n_gz):
                remote(
                    column_part.at[strip_of(g), :], column_in.at[gz(step)],
                    column_send.at[0], column_recv.at[gz(step)], gz=gz(step),
                ).wait_recv()
                total += column_in[gz(step)]
            panel[strip_of(g), :] = total
            for step in range(1, n_col):
                hand_copy(step).start()

    def column_gather():
        @pl.when(c != 0)
        def _():
            hand_copy(1).wait_recv()

        piece = panel.at[strip_of(g), :]
        for step in range(1, n_gz):
            start(remote(piece, piece, panel_send.at[step], panel_recv.at[g], gz=gz(step)))

    def panel_done():
        for step in range(1, n_gz):
            piece = panel.at[strip_of(gz(step)), :]
            remote(piece, piece, panel_send.at[0], panel_recv.at[gz(step)], gz=gz(step)).wait_recv()

        @pl.when(g != r)
        def _():
            spread_copy(1).wait_recv()

    done = [0]

    def factor_part(count):
        eliminate(done[0], count, worked, product, upper_unit, lower_inverse)
        done[0] += count

    def term_copy(j):
        span = pl.ds(pl.multiple_of(core * half, half), half)
        return remote(terms.at[j], arrived.at[x, span, :], term_send.at[j], term_recv.at[g], gz=j)

    def layer_rows(j, which):
        span = pl.ds(which * half, half)
        if not isinstance(which, int):
            span = pl.ds(pl.multiple_of(which * half, half), half)
        total = jnp.dot(lowers[0, span, :], gathered[j, 0], preferred_element_type=jnp.float32)
        for k_block in range(1, n_col):
            total += jnp.dot(
                lowers[k_block, span, :], gathered[j, k_block], preferred_element_type=jnp.float32
            )
        return total

    def pair_copy(j):
        return remote(pair_out.at[j], pair_in.at[j], pair_send.at[j], pair_recv.at[j], gz=sibling)

    def term(distance):
        j = row(distance)

        @pl.when((j != 0) | (c != 0))
        def _():
            pair_out[j] = layer_rows(j, 1 - core)
            pair_copy(j).start()
            terms[j] = layer_rows(j, core)

    def term_out(distance):
        j = row(distance)

        @pl.when((j != 0) | (c != 0))
        def _():
            pair_copy(j).wait_recv()
            terms[j] += pair_in[j]

            @pl.when(j != g)
            def _():
                term_copy(j).start()

            @pl.when(j == g)
            def _():
                arrived[x, pl.ds(pl.multiple_of(core * half, half), half), :] = terms[j]

    @pl.when(r == 0)
    def _():
        for step in range(1, n_col):
            pivot_split_copy(step).start()
        for at in range(2):
            chain(1, at).start()
            chain(-1, at).start()

    for slot, step in enumerate(ORDER_OF_K[1:]):
        start(
            remote(
                uppers.at[col(step)], gathered.at[r, c], up_send.at[slot], up_recv.at[c], col=col(step)
            )
        )
    z_step(0)
    for way in (1, -1):
        start(low_copy(way))

    @pl.when((r == 0) & (g != 0))
    def _():
        row_front_copy().start()

    def panels_out(upper_inverse):
        panel_done()
        upper = exact_dot(lower_inverse[...], row_panel[...])
        upper_panel[...] = upper
        for at in range(panels):
            span = pl.ds(at * BLOCK, BLOCK)
            lower = exact_dot(panel[span, :], upper_inverse)
            lower_panel[span, :] = lower
            kept = jnp.where(corner, panel[span, :], front[span, :])
            trailing[span, :] = kept - exact_dot(lower, upper)

    def far_arrive():
        far_wait(last + 1, 1, (0, 1))
        far_wait(last + 1, -1, (2, 3))

    pivot_over_col()
    z_step(1)
    chain_hop(1)
    z_step(2)
    pivot_over_gz()
    z_step(3)
    chain_hop(2)
    z_step(4)
    pivot_out()
    chain_hop(3)
    z_step(5)
    pivot_done()
    factor_part(8)
    chain_hop(4)
    row_products()
    factor_part(8)
    z_step(6)
    for way in (1, -1):
        low_pass(way)
    factor_part(8)
    z_step(7)
    row_over_col()
    factor_part(16)
    z_step(8)
    factor_part(16)
    z_step(9)
    row_over_gz()
    factor_part(16)
    z_step(10)
    factor_part(8)
    z_step(11)
    for way in (1, -1):
        low_far_wait(way)
    term(0)
    term(1)
    column_product()
    term(-1)
    term_out(0)
    term_out(1)
    z_step(12)
    factor_part(8)
    term_out(-1)
    column_over_gz()
    z_step(13)
    term(2)
    column_gather()
    term(-2)
    term_out(2)
    term_out(-2)
    far_wait(last, 1, (2, 3))
    far_wait(last, -1, (0, 1))
    term(3)
    term(-3)
    term_out(3)
    term_out(-3)
    far_arrive()
    term(4)
    term_out(4)
    factor_part(40)
    upper_inverse = finish_elimination(worked, upper_unit)
    panels_out(upper_inverse)

    @pl.when((g != 0) | (c != 0))
    def _():
        for step in range(1, n_gz):
            other = gz(step)
            span = pl.ds(pl.multiple_of(lax.rem(other, 2) * half, half), half)
            block = arrived.at[other // 2, span, :]
            remote(block, block, term_send.at[0], term_recv.at[other], gz=other).wait_recv()

        def add_up(at, carry):
            span = pl.ds(pl.multiple_of(at * BLOCK, BLOCK), BLOCK)
            total = arrived[0, span, :]
            for chip in range(1, n_gz // 2):
                total += arrived[chip, span, :]
            trailing[span, :] -= total
            return carry

        lax.fori_loop(0, panels, add_up, 0)

    for copy in sends:
        copy.wait_send()
    for step in range(n_gz):
        j = gz(step)

        @pl.when((j != 0) | (c != 0))
        def _():
            pair_copy(j).wait_send()
            if step:
                term_copy(j).wait_send()

    @pl.when(c == 0)
    def _():
        for step in range(1, n_gz):
            column_copy(step).wait_send()
        for step in range(1, n_col):
            hand_copy(step).wait_send()

    @pl.when(r < n_row // 2)
    def _():
        for at in range(2):
            chain(1, at).wait_send()

    @pl.when((r == 0) | (r > n_row // 2 + 1))
    def _():
        for at in range(2):
            chain(-1, at).wait_send()

    @pl.when(r == 0)
    def _():
        for step in range(1, n_col):
            pivot_split_copy(step).wait_send()
        for step in range(1, n_gz):
            pivot_sum_copy(step).wait_send()
        for step in range(1, n_row):
            pivot_row_copy(step).wait_send()

    @pl.when((r == 0) & (g != 0))
    def _():
        row_front_copy().wait_send()

    @pl.when(g != r)
    def _():
        row_copy().wait_send()

    @pl.when(g == r)
    def _():
        for step in range(1, n_row):
            spread_copy(step).wait_send()


def shards(n_gz, n_row, n_col, subtree_lower, subtree_upper, touched, front):
    height, depth = subtree_lower.shape[1:]
    width = front.shape[3]
    half = height // 2
    bf16, f32 = jnp.bfloat16, jnp.float32
    dma = pltpu.SemaphoreType.DMA
    backs = BLOCK // n_col
    vmem = pl.BlockSpec(memory_space=pltpu.VMEM)
    anywhere = pl.BlockSpec(memory_space=pltpu.HBM)
    lower_panel, upper_panel, trailing = pl.pallas_call(
        functools.partial(front_kernel, n_gz, n_row, n_col),
        out_shape=(
            jax.ShapeDtypeStruct((height, width), f32),
            jax.ShapeDtypeStruct((width, width), f32),
            jax.ShapeDtypeStruct((height, width), f32),
        ),
        in_specs=[anywhere] * 4,
        out_specs=(vmem, vmem, vmem),
        scratch_shapes=[
            pltpu.VMEM((height, depth), bf16),
            pltpu.VMEM((depth, height), bf16),
            pltpu.SMEM(touched.shape, jnp.int32),
            pltpu.VMEM((height, width), f32),
            pltpu.VMEM((n_col, height, depth), bf16),
            pltpu.VMEM((n_col, depth, BLOCK), bf16),
            pltpu.VMEM((n_row, n_col, depth, BLOCK), bf16),
            pltpu.VMEM((n_gz, half, BLOCK), f32),
            pltpu.VMEM((n_gz, half, BLOCK), f32),
            pltpu.VMEM((n_gz, half, BLOCK), f32),
            pltpu.VMEM((n_gz // 2, height, BLOCK), f32),
            pltpu.VMEM((BLOCK, depth), bf16),
            pltpu.VMEM((BLOCK, BLOCK), f32),
            pltpu.VMEM((n_col, backs, BLOCK), f32),
            pltpu.VMEM((n_col, backs, BLOCK), f32),
            pltpu.VMEM((backs, BLOCK), f32),
            pltpu.VMEM((n_gz, backs, BLOCK), f32),
            pltpu.VMEM((n_col, backs, BLOCK), f32),
            pltpu.VMEM((n_col, BLOCK, BLOCK), f32),
            pltpu.VMEM((n_col, BLOCK, BLOCK), f32),
            pltpu.VMEM((BLOCK, BLOCK), f32),
            pltpu.VMEM((n_gz, BLOCK, BLOCK), f32),
            pltpu.VMEM((BLOCK, BLOCK), f32),
            pltpu.VMEM((height, BLOCK), f32),
            pltpu.VMEM((n_gz, height // n_gz, BLOCK), f32),
            pltpu.VMEM((height, BLOCK), f32),
            pltpu.VMEM((BLOCK, BLOCK), f32),
            pltpu.VMEM((BLOCK, BLOCK), f32),
            pltpu.VMEM((BLOCK, BLOCK), f32),
            pltpu.VMEM((BLOCK, BLOCK), f32),
            dma((4,)),
            dma((n_col,)), dma((n_col,)),
            dma((4,)), dma((4,)),
            dma((2, len(NATURAL))), dma((n_row, n_col)),
            dma((n_gz,)), dma((n_gz,)),
            dma((n_gz,)), dma((n_gz,)),
            dma((2, 2)), dma((2,)),
            dma((2,)),
            dma((n_col,)), dma((n_col,)),
            dma((n_gz,)), dma((n_gz,)),
            dma((n_row,)), dma,
            dma((n_col,)), dma((n_col,)),
            dma((n_col,)), dma((n_col,)),
            dma, dma((n_gz,)),
            dma((n_row,)), dma,
            dma((n_gz,)), dma((n_gz,)),
            dma((n_col,)), dma,
            dma((n_gz,)), dma((n_gz,)),
        ],
        compiler_params=pltpu.CompilerParams(
            collective_id=0, has_side_effects=True, vmem_limit_bytes=63 * 1024 * 1024
        ),
    )(subtree_lower[0], subtree_upper[0], touched, front.reshape(height, width))
    return (
        lower_panel,
        upper_panel.reshape(width, 1, 1, width),
        trailing.reshape(height, 1, 1, width),
    )


def solution(mesh):
    placed = (
        P("gz", "row", "col"),
        P("gz", "col", "row"),
        P("gz", None),
        P("row", "gz", "col", None),
    )
    return jax.shard_map(
        functools.partial(shards, mesh.shape["gz"], mesh.shape["row"], mesh.shape["col"]),
        mesh=mesh,
        in_specs=placed,
        out_specs=(P("row", None), P(None, "gz", "col", None), P("row", "gz", "col", None)),
        check_vma=False,
    )
```

```python
import functools

import jax
import jax.numpy as jnp
from jax import lax
from jax.experimental import pallas as pl
from jax.experimental.pallas import tpu as pltpu
from jax.sharding import PartitionSpec as P

BLOCK = 128
GROUP = 4
MESH = pl.DeviceIdType.MESH
ORDER_OF_K = (0, 1, 3, 2)
NATURAL = [(away, place) for away in range(3) for place in range(4)] + [(3, 0), (3, 1)]
OWN, NEXT, FAR = NATURAL[0:4], NATURAL[4:8], NATURAL[8:12]
RING = {
    1: OWN[:2] + NEXT + OWN[2:] + FAR + [(3, 0), (3, 1)],
    2: OWN + FAR + NEXT + [(3, 0), (3, 1)],
    3: OWN + NEXT[:2] + [(3, 0), (3, 1)] + NEXT[2:] + FAR,
}
RING_BACK = {1: RING[1], 2: RING[2], 3: OWN + NEXT + [(3, 0), (3, 1)] + FAR}


def exact_dot(left, right):
    return jnp.dot(
        left, right, precision=lax.Precision.HIGHEST, preferred_element_type=jnp.float32
    )


def eliminate(first, count, worked, product, upper, lower_inverse):
    lanes = lax.broadcasted_iota(jnp.int32, (1, BLOCK), 1)
    rows = lax.broadcasted_iota(jnp.int32, (BLOCK, 1), 0)

    def step(group, carry):
        places = [group * GROUP + s for s in range(GROUP)]
        here = [lanes == place for place in places]
        dense, products, kept = worked[...], product[...], upper[...]
        pivot_rows = [worked[pl.ds(place, 1), :] for place in places]
        product_rows = [product[pl.ds(place, 1), :] for place in places]

        def take(values, hit):
            return jnp.sum(jnp.where(hit, values, 0.0), axis=1, keepdims=True)

        columns = [take(dense, hit) for hit in here]
        corner = [[take(line, hit) for hit in here] for line in pivot_rows]
        scaled = []
        for s in range(GROUP):
            inverse = 1.0 / corner[s][s]
            factors = jnp.where(rows == places[s], 0.0, columns[s] * inverse)
            for u in range(s + 1, GROUP):
                ratio = corner[u][s] * inverse
                pivot_rows[u] = pivot_rows[u] - ratio * pivot_rows[s]
                product_rows[u] = product_rows[u] - ratio * product_rows[s]
                for t in range(s + 1, GROUP):
                    corner[u][t] = corner[u][t] - ratio * corner[s][t]
            for t in range(s + 1, GROUP):
                columns[t] = columns[t] - factors * corner[s][t]
            scaled.append(factors)
        for s in range(GROUP):
            lower_inverse[pl.ds(places[s], 1), :] = product_rows[s]
            dense = dense - scaled[s] * pivot_rows[s]
            products = products - scaled[s] * product_rows[s]
            kept = jnp.where(here[s], -scaled[s], kept)
        worked[...] = dense
        product[...] = products
        upper[...] = kept
        return carry

    lax.fori_loop(first // GROUP, (first + count) // GROUP, step, 0)


def start_elimination(pivot, worked, product, upper):
    rows = lax.broadcasted_iota(jnp.int32, (BLOCK, BLOCK), 0)
    lanes = lax.broadcasted_iota(jnp.int32, (BLOCK, BLOCK), 1)
    identity = jnp.where(rows == lanes, 1.0, 0.0)
    worked[...] = pivot
    product[...] = identity
    upper[...] = identity


def finish_elimination(worked, upper):
    rows = lax.broadcasted_iota(jnp.int32, (BLOCK, BLOCK), 0)
    lanes = lax.broadcasted_iota(jnp.int32, (BLOCK, BLOCK), 1)
    pivots = jnp.sum(jnp.where(rows == lanes, worked[...], 0.0), axis=1, keepdims=True)
    unit = jnp.where(rows < lanes, upper[...], jnp.where(rows == lanes, 1.0, 0.0))
    return unit / pivots


def remote(src, dst, send_sem, recv_sem, **where):
    return pltpu.make_async_remote_copy(
        src_ref=src,
        dst_ref=dst,
        send_sem=send_sem,
        recv_sem=recv_sem,
        device_id=where,
        device_id_type=MESH,
    )


def front_kernel(
    n_gz, n_row, n_col,
    lower_hbm, upper_hbm, touched_hbm, front_hbm,
    lower_panel, upper_panel, trailing,
    lower_in, upper_in, touched, front,
    lowers, uppers, gathered, terms, pair_out, pair_in, arrived,
    first_rows, row_front,
    pivot_split, pivot_split_in, pivot_sum, pivot_sum_in, pivot,
    split, split_in, summed, row_in, row_panel, column_part, column_in, panel,
    worked, product, upper_unit, lower_inverse,
    in_sem, up_send, up_recv, low_send, low_recv, z_send, z_recv, term_send, term_recv,
    pair_send, pair_recv, chain_send, chain_recv, row_front_sem,
    pivot_split_send, pivot_split_recv, pivot_sum_send, pivot_sum_recv,
    pivot_row_send, pivot_row_recv, pivot_col_send, pivot_col_recv,
    split_send, split_recv, row_send, row_recv, spread_send, spread_recv,
    column_send, column_recv, hand_send, hand_recv, panel_send, panel_recv,
):
    g, r, c = lax.axis_index("gz"), lax.axis_index("row"), lax.axis_index("col")
    height = lower_in.shape[0]
    panels = height // BLOCK
    half = height // 2
    backs = BLOCK // n_col
    x, core = g // 2, lax.rem(g, 2)
    sibling = g + 1 - 2 * core
    sends = []

    def gz(step):
        return lax.rem(g + step, n_gz)

    def row(step):
        return lax.rem(r + n_row + step, n_row)

    def col(step):
        return lax.rem(c + n_col + step, n_col)

    def start(copy):
        copy.start()
        sends.append(copy)

    inputs = [
        pltpu.make_async_copy(upper_hbm, upper_in, in_sem.at[0]),
        pltpu.make_async_copy(touched_hbm, touched, in_sem.at[1]),
        pltpu.make_async_copy(lower_hbm, lower_in, in_sem.at[2]),
        pltpu.make_async_copy(front_hbm, front, in_sem.at[3]),
    ]
    for copy in inputs:
        copy.start()

    barrier = pltpu.get_barrier_semaphore()
    for step in range(1, n_gz):
        pl.semaphore_signal(barrier, inc=1, device_id={"gz": gz(step)}, device_id_type=MESH)
    for step in range(1, n_row):
        pl.semaphore_signal(barrier, inc=1, device_id={"row": row(step)}, device_id_type=MESH)
    for step in range(1, n_col):
        pl.semaphore_signal(barrier, inc=1, device_id={"col": col(step)}, device_id_type=MESH)

    for copy in inputs:
        copy.wait()
    for at in range(panels):
        mark = touched[0, r * panels + at].astype(jnp.float32)
        span = pl.ds(at * BLOCK, BLOCK)
        uppers[at] = (upper_in[:, span].astype(jnp.float32) * mark).astype(jnp.bfloat16)
        lowers[c, span, :] = (lower_in[span, :].astype(jnp.float32) * mark).astype(jnp.bfloat16)
    gathered[0, c, :, :BLOCK] = uppers[c]
    corner = (g == 0) & (c == 0)
    strip = height // n_gz

    @pl.when(r == 0)
    def _():
        first_rows[...] = lowers[c, :BLOCK, :]
        part = -jnp.dot(lowers[c, :BLOCK, :], uppers[0], preferred_element_type=jnp.float32)
        for at in range(n_col):
            pivot_split[at] = part[at * backs : (at + 1) * backs]

    @pl.when((r == 0) & (g == 0))
    def _():
        row_front[...] = front[:BLOCK, :]

    @pl.when((r == 0) & corner)
    def _():
        for at in range(n_col):
            pivot_split[at] += front[at * backs : (at + 1) * backs, :]

    pl.semaphore_wait(barrier, n_gz + n_row + n_col - 3)

    def pivot_split_copy(step):
        return remote(
            pivot_split.at[col(step)], pivot_split_in.at[c],
            pivot_split_send.at[step], pivot_split_recv.at[c], col=col(step),
        )

    def pivot_sum_copy(step):
        return remote(
            pivot_sum, pivot_sum_in.at[g], pivot_sum_send.at[step], pivot_sum_recv.at[g], gz=gz(step)
        )

    def pivot_row_copy(step):
        piece = pivot.at[c]
        return remote(piece, piece, pivot_row_send.at[step], pivot_row_recv, row=row(step))

    def pivot_over_col():
        @pl.when(r == 0)
        def _():
            for step in range(1, n_col):
                remote(
                    pivot_split.at[0], pivot_split_in.at[col(step)],
                    pivot_split_send.at[0], pivot_split_recv.at[col(step)], col=col(step),
                ).wait_recv()
            total = pivot_split[c]
            for step in range(1, n_col):
                total += pivot_split_in[col(step)]
            pivot_sum[...] = total
            for step in range(1, n_gz):
                pivot_sum_copy(step).start()

    def pivot_over_gz():
        @pl.when(r == 0)
        def _():
            for step in range(1, n_gz):
                remote(
                    pivot_sum, pivot_sum_in.at[gz(step)],
                    pivot_sum_send.at[0], pivot_sum_recv.at[gz(step)], gz=gz(step),
                ).wait_recv()
            total = pivot_sum[...]
            for step in range(1, n_gz):
                total += pivot_sum_in[gz(step)]
            pivot[c] = total
            for step in range(1, n_row):
                pivot_row_copy(step).start()

    def pivot_out():
        @pl.when(r != 0)
        def _():
            pivot_row_copy(1).wait_recv()

        for step in range(1, n_col):
            piece = pivot.at[c]
            start(remote(piece, piece, pivot_col_send.at[step], pivot_col_recv.at[c], col=col(step)))

    def pivot_done():
        for step in range(1, n_col):
            piece = pivot.at[col(step)]
            remote(
                piece, piece, pivot_col_send.at[0], pivot_col_recv.at[col(step)], col=col(step)
            ).wait_recv()
        whole = jnp.concatenate([pivot[at] for at in range(n_col)], axis=0)
        start_elimination(whole, worked, product, upper_unit)

    def chain(way, at):
        slot = 0 if way > 0 else 1
        piece = first_rows.at[pl.ds(at * (BLOCK // 2), BLOCK // 2), :]
        return remote(piece, piece, chain_send.at[slot, at], chain_recv.at[at], row=row(way))

    def chain_hop(hop):
        def pass_on(way):
            for at in range(2):
                chain(1, at).wait_recv()
                if way:
                    chain(way, at).start()

        @pl.when(r == hop)
        def _():
            pass_on(1 if hop < n_row // 2 else 0)

        if hop < n_row // 2:
            @pl.when(r == n_row - hop)
            def _():
                pass_on(-1 if hop < n_row // 2 - 1 else 0)

    def row_front_copy():
        return remote(
            front.at[pl.ds(0, BLOCK), :], row_front, row_front_sem.at[0], row_front_sem.at[1], row=g
        )

    def side(way):
        return pl.ds(0 if way > 0 else BLOCK, BLOCK)

    def up_arrive(step):
        block = gathered.at[0, col(step), :, side(1)]
        remote(uppers.at[0], block, up_send.at[0], up_recv.at[col(step)], col=col(step)).wait_recv()

    def z_wait(distance, way, place):
        k_block = col(ORDER_OF_K[place])
        slot = 0 if way > 0 else 1
        piece = gathered.at[distance, k_block, :, side(way)]
        remote(
            piece, piece, z_send.at[0, 0], z_recv.at[distance, slot, k_block], row=row(1)
        ).wait_recv()

    last = n_row // 2 - 1

    def ring_entry(way, at):
        def entry(order):
            away, place = order[at]
            if away == last and way < 0:
                place += n_col // 2
            return away, ORDER_OF_K[place]

        from_first = r if way > 0 else lax.rem(n_row - r, n_row)
        away, offset = entry(NATURAL)
        if all(entry(order) == (away, offset) for order in (RING if way > 0 else RING_BACK).values()):
            return away, offset
        for distance, order in (RING if way > 0 else RING_BACK).items():
            here = from_first == distance
            away = jnp.where(here, entry(order)[0], away)
            offset = jnp.where(here, entry(order)[1], offset)
        return away, offset

    def z_step(at):
        if 0 < at < n_col:
            up_arrive(ORDER_OF_K[at])
        for way in (1, -1):
            away, offset = ring_entry(way, at)
            k_block = col(offset)
            slot = 0 if way > 0 else 1
            lanes = side(way)
            if way < 0:
                start_lane = jnp.where(away == 0, 0, BLOCK)
                lanes = pl.ds(pl.multiple_of(start_lane, BLOCK), BLOCK)
            copy = remote(
                gathered.at[away, k_block, :, lanes], gathered.at[away + 1, k_block, :, side(way)],
                z_send.at[slot, at], z_recv.at[away + 1, slot, k_block], row=row(way),
            )
            arrived_here = gathered.at[away, k_block, :, lanes]
            arrival = remote(
                arrived_here, arrived_here, z_send.at[slot, at], z_recv.at[away, slot, k_block], row=row(way)
            )
            if not isinstance(away, int):
                pl.when(away > 0)(arrival.wait_recv)
            elif away > 0:
                arrival.wait_recv()
            start(copy)

    def far_wait(distance, way, places):
        @pl.when(row(-way * distance) != 0)
        def _():
            for place in places:
                z_wait(distance, way, place)

    def half_of(at):
        return pl.ds(at * half, half)

    def low_copy(way, second):
        slot = 0 if way > 0 else 1
        piece = lowers.at[c, half_of(1 - slot if second else slot), :]
        at = 4 + slot if second else slot
        return remote(piece, piece, low_send.at[at], low_recv.at[at], col=col(way))

    def low_start(second):
        for way in (1, -1):
            start(low_copy(way, second))

    def low_pass():
        for way in (1, -1):
            slot = 0 if way > 0 else 1
            piece = lowers.at[col(-way), half_of(slot), :]
            remote(piece, piece, low_send.at[slot], low_recv.at[slot], col=col(way)).wait_recv()
            start(remote(piece, piece, low_send.at[2 + slot], low_recv.at[2 + slot], col=col(way)))

    def low_done():
        for way in (1, -1):
            slot = 0 if way > 0 else 1
            piece = lowers.at[col(-way), half_of(1 - slot), :]
            remote(piece, piece, low_send.at[4 + slot], low_recv.at[4 + slot], col=col(way)).wait_recv()
            piece = lowers.at[col(2), half_of(slot), :]
            remote(piece, piece, low_send.at[2 + slot], low_recv.at[2 + slot], col=col(way)).wait_recv()

    def row_products():
        for at in range(n_col):
            split[at] = -jnp.dot(first_rows[...], uppers[at], preferred_element_type=jnp.float32)
        for step in range(1, n_col):
            start(
                remote(
                    split.at[col(step)], split_in.at[c],
                    split_send.at[step], split_recv.at[c], col=col(step),
                )
            )

    def row_copy():
        return remote(summed, row_in.at[g], row_send, row_recv.at[g], gz=r)

    def row_over_col():
        for step in range(1, n_col):
            remote(
                split.at[0], split_in.at[col(step)],
                split_send.at[0], split_recv.at[col(step)], col=col(step),
            ).wait_recv()
        total = split[c]
        for step in range(1, n_col):
            total += split_in[col(step)]
        summed[...] = total

        @pl.when(g != r)
        def _():
            row_copy().start()

    def spread_copy(step):
        return remote(row_panel, row_panel, spread_send.at[step], spread_recv, row=row(step))

    def row_over_gz():
        @pl.when(g == r)
        def _():
            @pl.when(g != 0)
            def _():
                row_front_copy().wait_recv()

            total = summed[...] + row_front[...]
            for step in range(1, n_gz):
                remote(
                    summed, row_in.at[gz(step)], row_send, row_recv.at[gz(step)], gz=gz(step)
                ).wait_recv()
                total += row_in[gz(step)]
            row_panel[...] = total
            for step in range(1, n_row):
                spread_copy(step).start()

    def strip_of(at):
        return pl.ds(pl.multiple_of(at * strip, strip), strip)

    def column_copy(step):
        return remote(
            column_part.at[strip_of(gz(step)), :], column_in.at[g],
            column_send.at[step], column_recv.at[g], gz=gz(step),
        )

    def hand_copy(step):
        piece = panel.at[strip_of(g), :]
        return remote(piece, piece, hand_send.at[step], hand_recv, col=col(step))

    def column_product():
        far = n_row // 2
        for plane, waits in (
            (far - 1, ((1, 2), (1, 3))),
            (far, ((1, 0), (1, 1), (-1, 2), (-1, 3))),
            (far + 1, ((-1, 0), (-1, 1))),
        ):
            @pl.when(r == plane)
            def _():
                for way, place in waits:
                    z_wait(min(plane, n_row - plane), way, place)

        distance = jnp.where(r <= far, r, n_row - r)

        def first_block(place):
            up = (r < far) | ((r == far) & (place < 2))
            lanes = pl.ds(pl.multiple_of(jnp.where(up, 0, BLOCK), BLOCK), BLOCK)
            return gathered[distance, col(ORDER_OF_K[place]), :, lanes]

        @pl.when(c == 0)
        def _():
            for which in range(2):
                column_part[which * half : (which + 1) * half, :] = -layer_rows(first_block, which)

            @pl.when(g == 0)
            def _():
                column_part[...] += front[...]

            for step in range(1, n_gz):
                column_copy(step).start()

    def column_over_gz():
        @pl.when(c == 0)
        def _():
            total = column_part[strip_of(g), :]
            for step in range(1, n_gz):
                remote(
                    column_part.at[strip_of(g), :], column_in.at[gz(step)],
                    column_send.at[0], column_recv.at[gz(step)], gz=gz(step),
                ).wait_recv()
                total += column_in[gz(step)]
            panel[strip_of(g), :] = total
            for step in range(1, n_col):
                hand_copy(step).start()

    def column_gather():
        @pl.when(c != 0)
        def _():
            hand_copy(1).wait_recv()

        piece = panel.at[strip_of(g), :]
        for step in range(1, n_gz):
            start(remote(piece, piece, panel_send.at[step], panel_recv.at[g], gz=gz(step)))

    def panel_done():
        for step in range(1, n_gz):
            piece = panel.at[strip_of(gz(step)), :]
            remote(piece, piece, panel_send.at[0], panel_recv.at[gz(step)], gz=gz(step)).wait_recv()

        @pl.when(g != r)
        def _():
            spread_copy(1).wait_recv()

    done = [0]

    def factor_part(count):
        eliminate(done[0], count, worked, product, upper_unit, lower_inverse)
        done[0] += count

    def term_copy(j):
        span = pl.ds(pl.multiple_of(core * half, half), half)
        return remote(terms.at[j], arrived.at[x, span, :], term_send.at[j], term_recv.at[g], gz=j)

    def layer_rows(block, which):
        span = pl.ds(which * half, half)
        if not isinstance(which, int):
            span = pl.ds(pl.multiple_of(which * half, half), half)
        total = None
        for place in range(n_col):
            k_block = col(ORDER_OF_K[place])
            part = jnp.dot(lowers[k_block, span, :], block(place), preferred_element_type=jnp.float32)
            total = part if total is None else total + part
        return total

    def pair_copy(j):
        return remote(pair_out.at[j], pair_in.at[j], pair_send.at[j], pair_recv.at[j], gz=sibling)

    def term(distance):
        def block(place):
            k_block = col(ORDER_OF_K[place])
            if 0 < distance <= last:
                return gathered[distance, k_block]
            return gathered[distance, k_block, :, side(1 if distance == 0 or place < 2 else -1)]

        ends = (row(-distance), row(distance)) if 0 < distance <= last else (row(distance),)

        def put(where, values, send):
            for at, j in enumerate(ends):
                @pl.when((j != 0) | (c != 0))
                def _():
                    where[j] = values[:, at * BLOCK : (at + 1) * BLOCK]
                    if send:
                        pair_copy(j).start()

        put(pair_out, layer_rows(block, 1 - core), True)
        put(terms, layer_rows(block, core), False)

    def term_out(distance):
        j = row(distance)

        @pl.when((j != 0) | (c != 0))
        def _():
            pair_copy(j).wait_recv()
            terms[j] += pair_in[j]

            @pl.when(j != g)
            def _():
                term_copy(j).start()

            @pl.when(j == g)
            def _():
                arrived[x, pl.ds(pl.multiple_of(core * half, half), half), :] = terms[j]

    @pl.when(r == 0)
    def _():
        for step in range(1, n_col):
            pivot_split_copy(step).start()
        for at in range(2):
            chain(1, at).start()
            chain(-1, at).start()

    for slot, step in enumerate(ORDER_OF_K[1:]):
        mine = gathered.at[0, c, :, side(1)]
        start(remote(uppers.at[col(step)], mine, up_send.at[slot], up_recv.at[c], col=col(step)))
    z_step(0)
    low_start(False)

    @pl.when((r == 0) & (g != 0))
    def _():
        row_front_copy().start()

    def panels_out(upper_inverse):
        panel_done()
        upper = exact_dot(lower_inverse[...], row_panel[...])
        upper_panel[...] = upper
        for at in range(panels):
            span = pl.ds(at * BLOCK, BLOCK)
            lower = exact_dot(panel[span, :], upper_inverse)
            lower_panel[span, :] = lower
            kept = jnp.where(corner, panel[span, :], front[span, :])
            trailing[span, :] = kept - exact_dot(lower, upper)

    def far_arrive():
        far_wait(last + 1, 1, (0, 1))
        far_wait(last + 1, -1, (2, 3))

    pivot_over_col()
    z_step(1)
    chain_hop(1)
    z_step(2)
    low_start(True)
    pivot_over_gz()
    z_step(3)
    chain_hop(2)
    z_step(4)
    pivot_out()
    low_pass()
    chain_hop(3)
    z_step(5)
    pivot_done()
    factor_part(8)
    chain_hop(4)
    row_products()
    factor_part(8)
    z_step(6)
    factor_part(8)
    z_step(7)
    row_over_col()
    factor_part(16)
    z_step(8)
    factor_part(16)
    z_step(9)
    row_over_gz()
    low_done()
    term(0)
    factor_part(8)
    z_step(10)
    column_product()
    term_out(0)
    factor_part(16)
    z_step(11)
    term(1)
    column_over_gz()
    term_out(1)
    term_out(-1)
    z_step(12)
    column_gather()
    factor_part(8)
    z_step(13)
    term(2)
    term_out(2)
    term_out(-2)
    far_wait(last, 1, (2, 3))
    far_wait(last, -1, (0, 1))
    term(3)
    term_out(3)
    term_out(-3)
    far_arrive()
    term(4)
    term_out(4)
    factor_part(40)
    upper_inverse = finish_elimination(worked, upper_unit)
    panels_out(upper_inverse)

    @pl.when((g != 0) | (c != 0))
    def _():
        for step in range(1, n_gz):
            other = gz(step)
            span = pl.ds(pl.multiple_of(lax.rem(other, 2) * half, half), half)
            block = arrived.at[other // 2, span, :]
            remote(block, block, term_send.at[0], term_recv.at[other], gz=other).wait_recv()

        def add_up(at, carry):
            span = pl.ds(pl.multiple_of(at * BLOCK, BLOCK), BLOCK)
            total = arrived[0, span, :]
            for chip in range(1, n_gz // 2):
                total += arrived[chip, span, :]
            trailing[span, :] -= total
            return carry

        lax.fori_loop(0, panels, add_up, 0)

    for copy in sends:
        copy.wait_send()
    for step in range(n_gz):
        j = gz(step)

        @pl.when((j != 0) | (c != 0))
        def _():
            pair_copy(j).wait_send()
            if step:
                term_copy(j).wait_send()

    @pl.when(c == 0)
    def _():
        for step in range(1, n_gz):
            column_copy(step).wait_send()
        for step in range(1, n_col):
            hand_copy(step).wait_send()

    @pl.when(r < n_row // 2)
    def _():
        for at in range(2):
            chain(1, at).wait_send()

    @pl.when((r == 0) | (r > n_row // 2 + 1))
    def _():
        for at in range(2):
            chain(-1, at).wait_send()

    @pl.when(r == 0)
    def _():
        for step in range(1, n_col):
            pivot_split_copy(step).wait_send()
        for step in range(1, n_gz):
            pivot_sum_copy(step).wait_send()
        for step in range(1, n_row):
            pivot_row_copy(step).wait_send()

    @pl.when((r == 0) & (g != 0))
    def _():
        row_front_copy().wait_send()

    @pl.when(g != r)
    def _():
        row_copy().wait_send()

    @pl.when(g == r)
    def _():
        for step in range(1, n_row):
            spread_copy(step).wait_send()


def shards(n_gz, n_row, n_col, subtree_lower, subtree_upper, touched, front):
    height, depth = subtree_lower.shape[1:]
    width = front.shape[3]
    half = height // 2
    bf16, f32 = jnp.bfloat16, jnp.float32
    dma = pltpu.SemaphoreType.DMA
    backs = BLOCK // n_col
    vmem = pl.BlockSpec(memory_space=pltpu.VMEM)
    anywhere = pl.BlockSpec(memory_space=pltpu.HBM)
    lower_panel, upper_panel, trailing = pl.pallas_call(
        functools.partial(front_kernel, n_gz, n_row, n_col),
        out_shape=(
            jax.ShapeDtypeStruct((height, width), f32),
            jax.ShapeDtypeStruct((width, width), f32),
            jax.ShapeDtypeStruct((height, width), f32),
        ),
        in_specs=[anywhere] * 4,
        out_specs=(vmem, vmem, vmem),
        scratch_shapes=[
            pltpu.VMEM((height, depth), bf16),
            pltpu.VMEM((depth, height), bf16),
            pltpu.SMEM(touched.shape, jnp.int32),
            pltpu.VMEM((height, width), f32),
            pltpu.VMEM((n_col, height, depth), bf16),
            pltpu.VMEM((n_col, depth, BLOCK), bf16),
            pltpu.VMEM((n_row // 2 + 1, n_col, depth, 2 * BLOCK), bf16),
            pltpu.VMEM((n_gz, half, BLOCK), f32),
            pltpu.VMEM((n_gz, half, BLOCK), f32),
            pltpu.VMEM((n_gz, half, BLOCK), f32),
            pltpu.VMEM((n_gz // 2, height, BLOCK), f32),
            pltpu.VMEM((BLOCK, depth), bf16),
            pltpu.VMEM((BLOCK, BLOCK), f32),
            pltpu.VMEM((n_col, backs, BLOCK), f32),
            pltpu.VMEM((n_col, backs, BLOCK), f32),
            pltpu.VMEM((backs, BLOCK), f32),
            pltpu.VMEM((n_gz, backs, BLOCK), f32),
            pltpu.VMEM((n_col, backs, BLOCK), f32),
            pltpu.VMEM((n_col, BLOCK, BLOCK), f32),
            pltpu.VMEM((n_col, BLOCK, BLOCK), f32),
            pltpu.VMEM((BLOCK, BLOCK), f32),
            pltpu.VMEM((n_gz, BLOCK, BLOCK), f32),
            pltpu.VMEM((BLOCK, BLOCK), f32),
            pltpu.VMEM((height, BLOCK), f32),
            pltpu.VMEM((n_gz, height // n_gz, BLOCK), f32),
            pltpu.VMEM((height, BLOCK), f32),
            pltpu.VMEM((BLOCK, BLOCK), f32),
            pltpu.VMEM((BLOCK, BLOCK), f32),
            pltpu.VMEM((BLOCK, BLOCK), f32),
            pltpu.VMEM((BLOCK, BLOCK), f32),
            dma((4,)),
            dma((n_col,)), dma((n_col,)),
            dma((6,)), dma((6,)),
            dma((2, len(NATURAL))), dma((n_row // 2 + 1, 2, n_col)),
            dma((n_gz,)), dma((n_gz,)),
            dma((n_gz,)), dma((n_gz,)),
            dma((2, 2)), dma((2,)),
            dma((2,)),
            dma((n_col,)), dma((n_col,)),
            dma((n_gz,)), dma((n_gz,)),
            dma((n_row,)), dma,
            dma((n_col,)), dma((n_col,)),
            dma((n_col,)), dma((n_col,)),
            dma, dma((n_gz,)),
            dma((n_row,)), dma,
            dma((n_gz,)), dma((n_gz,)),
            dma((n_col,)), dma,
            dma((n_gz,)), dma((n_gz,)),
        ],
        compiler_params=pltpu.CompilerParams(
            collective_id=0, has_side_effects=True, vmem_limit_bytes=213 * 256 * 1024
        ),
    )(subtree_lower[0], subtree_upper[0], touched, front.reshape(height, width))
    return (
        lower_panel,
        upper_panel.reshape(width, 1, 1, width),
        trailing.reshape(height, 1, 1, width),
    )


def solution(mesh):
    placed = (
        P("gz", "row", "col"),
        P("gz", "col", "row"),
        P("gz", None),
        P("row", "gz", "col", None),
    )
    return jax.shard_map(
        functools.partial(shards, mesh.shape["gz"], mesh.shape["row"], mesh.shape["col"]),
        mesh=mesh,
        in_specs=placed,
        out_specs=(P("row", None), P(None, "gz", "col", None), P("row", "gz", "col", None)),
        check_vma=False,
    )
```

```python
import functools

import jax
import jax.numpy as jnp
from jax import lax
from jax.experimental import pallas as pl
from jax.experimental.pallas import tpu as pltpu
from jax.sharding import PartitionSpec as P

BLOCK = 128
GROUP = 4
MESH = pl.DeviceIdType.MESH
ORDER_OF_K = (0, 1, 3, 2)
NATURAL = [(away, place) for away in range(3) for place in range(4)] + [(3, 0), (3, 1)]
OWN, NEXT, FAR = NATURAL[0:4], NATURAL[4:8], NATURAL[8:12]
RING = {
    1: OWN[:2] + NEXT + OWN[2:] + FAR + [(3, 0), (3, 1)],
    2: OWN + FAR + NEXT + [(3, 0), (3, 1)],
    3: OWN + NEXT[:2] + [(3, 0), (3, 1)] + NEXT[2:] + FAR,
}
RING_BACK = {1: RING[1], 2: RING[2], 3: OWN + NEXT + [(3, 0), (3, 1)] + FAR}


def exact_dot(left, right):
    return jnp.dot(
        left, right, precision=lax.Precision.HIGHEST, preferred_element_type=jnp.float32
    )


def eliminate(first, count, worked, product, upper, lower_inverse):
    lanes = lax.broadcasted_iota(jnp.int32, (1, BLOCK), 1)
    rows = lax.broadcasted_iota(jnp.int32, (BLOCK, 1), 0)

    def step(group, carry):
        places = [group * GROUP + s for s in range(GROUP)]
        here = [lanes == place for place in places]
        dense, products, kept = worked[...], product[...], upper[...]
        pivot_rows = [worked[pl.ds(place, 1), :] for place in places]
        product_rows = [product[pl.ds(place, 1), :] for place in places]

        def take(values, hit):
            return jnp.sum(jnp.where(hit, values, 0.0), axis=1, keepdims=True)

        columns = [take(dense, hit) for hit in here]
        corner = [[take(line, hit) for hit in here] for line in pivot_rows]
        scaled = []
        for s in range(GROUP):
            inverse = 1.0 / corner[s][s]
            factors = jnp.where(rows == places[s], 0.0, columns[s] * inverse)
            for u in range(s + 1, GROUP):
                ratio = corner[u][s] * inverse
                pivot_rows[u] = pivot_rows[u] - ratio * pivot_rows[s]
                product_rows[u] = product_rows[u] - ratio * product_rows[s]
                for t in range(s + 1, GROUP):
                    corner[u][t] = corner[u][t] - ratio * corner[s][t]
            for t in range(s + 1, GROUP):
                columns[t] = columns[t] - factors * corner[s][t]
            scaled.append(factors)
        for s in range(GROUP):
            lower_inverse[pl.ds(places[s], 1), :] = product_rows[s]
            dense = dense - scaled[s] * pivot_rows[s]
            products = products - scaled[s] * product_rows[s]
            kept = jnp.where(here[s], -scaled[s], kept)
        worked[...] = dense
        product[...] = products
        upper[...] = kept
        return carry

    lax.fori_loop(first // GROUP, (first + count) // GROUP, step, 0)


def start_elimination(pivot, worked, product, upper):
    rows = lax.broadcasted_iota(jnp.int32, (BLOCK, BLOCK), 0)
    lanes = lax.broadcasted_iota(jnp.int32, (BLOCK, BLOCK), 1)
    identity = jnp.where(rows == lanes, 1.0, 0.0)
    worked[...] = pivot
    product[...] = identity
    upper[...] = identity


def finish_elimination(worked, upper):
    rows = lax.broadcasted_iota(jnp.int32, (BLOCK, BLOCK), 0)
    lanes = lax.broadcasted_iota(jnp.int32, (BLOCK, BLOCK), 1)
    pivots = jnp.sum(jnp.where(rows == lanes, worked[...], 0.0), axis=1, keepdims=True)
    unit = jnp.where(rows < lanes, upper[...], jnp.where(rows == lanes, 1.0, 0.0))
    return unit / pivots


def remote(src, dst, send_sem, recv_sem, **where):
    return pltpu.make_async_remote_copy(
        src_ref=src,
        dst_ref=dst,
        send_sem=send_sem,
        recv_sem=recv_sem,
        device_id=where,
        device_id_type=MESH,
    )


def front_kernel(
    n_gz, n_row, n_col,
    lower_hbm, upper_hbm, touched_hbm, front_hbm,
    lower_panel, upper_panel, trailing,
    lower_in, upper_in, touched, front,
    lowers, uppers, gathered, terms, pair_out, pair_in, arrived,
    first_rows, row_front,
    pivot_split, pivot_split_in, pivot_sum, pivot_sum_in, pivot,
    split, split_in, summed, row_in, row_panel, column_part, column_in, panel,
    worked, product, upper_unit, lower_inverse,
    in_sem, up_send, up_recv, low_send, low_recv, z_send, z_recv, term_send, term_recv,
    pair_send, pair_recv, chain_send, chain_recv, row_front_sem,
    pivot_split_send, pivot_split_recv, pivot_sum_send, pivot_sum_recv,
    pivot_row_send, pivot_row_recv, pivot_col_send, pivot_col_recv,
    split_send, split_recv, row_send, row_recv, spread_send, spread_recv,
    column_send, column_recv, hand_send, hand_recv, panel_send, panel_recv,
):
    g, r, c = lax.axis_index("gz"), lax.axis_index("row"), lax.axis_index("col")
    height = lower_in.shape[0]
    panels = height // BLOCK
    half = height // 2
    backs = BLOCK // n_col
    x, core = g // 2, lax.rem(g, 2)
    sibling = g + 1 - 2 * core
    sends = []

    def gz(step):
        return lax.rem(g + step, n_gz)

    def row(step):
        return lax.rem(r + n_row + step, n_row)

    def col(step):
        return lax.rem(c + n_col + step, n_col)

    def start(copy):
        copy.start()
        sends.append(copy)

    inputs = [
        pltpu.make_async_copy(upper_hbm, upper_in, in_sem.at[0]),
        pltpu.make_async_copy(touched_hbm, touched, in_sem.at[1]),
        pltpu.make_async_copy(lower_hbm, lower_in, in_sem.at[2]),
        pltpu.make_async_copy(front_hbm, front, in_sem.at[3]),
    ]
    for copy in inputs:
        copy.start()

    barrier = pltpu.get_barrier_semaphore()
    for step in range(1, n_gz):
        pl.semaphore_signal(barrier, inc=1, device_id={"gz": gz(step)}, device_id_type=MESH)
    for step in range(1, n_row):
        pl.semaphore_signal(barrier, inc=1, device_id={"row": row(step)}, device_id_type=MESH)
    for step in range(1, n_col):
        pl.semaphore_signal(barrier, inc=1, device_id={"col": col(step)}, device_id_type=MESH)

    for copy in inputs:
        copy.wait()
    for at in range(panels):
        mark = touched[0, r * panels + at].astype(jnp.float32)
        span = pl.ds(at * BLOCK, BLOCK)
        uppers[at] = (upper_in[:, span].astype(jnp.float32) * mark).astype(jnp.bfloat16)
        lowers[c, span, :] = (lower_in[span, :].astype(jnp.float32) * mark).astype(jnp.bfloat16)
    gathered[0, c, :, :BLOCK] = uppers[c]
    corner = (g == 0) & (c == 0)
    strip = height // n_gz

    @pl.when(r == 0)
    def _():
        first_rows[...] = lowers[c, :BLOCK, :]
        part = -jnp.dot(lowers[c, :BLOCK, :], uppers[0], preferred_element_type=jnp.float32)
        for at in range(n_col):
            pivot_split[at] = part[at * backs : (at + 1) * backs]

    @pl.when((r == 0) & (g == 0))
    def _():
        row_front[...] = front[:BLOCK, :]

    @pl.when((r == 0) & corner)
    def _():
        for at in range(n_col):
            pivot_split[at] += front[at * backs : (at + 1) * backs, :]

    pl.semaphore_wait(barrier, n_gz + n_row + n_col - 3)

    def pivot_split_copy(step):
        return remote(
            pivot_split.at[col(step)], pivot_split_in.at[c],
            pivot_split_send.at[step], pivot_split_recv.at[c], col=col(step),
        )

    def pivot_sum_copy(step):
        return remote(
            pivot_sum, pivot_sum_in.at[g], pivot_sum_send.at[step], pivot_sum_recv.at[g], gz=gz(step)
        )

    def pivot_row_copy(step):
        piece = pivot.at[c]
        return remote(piece, piece, pivot_row_send.at[step], pivot_row_recv, row=row(step))

    def pivot_over_col():
        @pl.when(r == 0)
        def _():
            for step in range(1, n_col):
                remote(
                    pivot_split.at[0], pivot_split_in.at[col(step)],
                    pivot_split_send.at[0], pivot_split_recv.at[col(step)], col=col(step),
                ).wait_recv()
            total = pivot_split[c]
            for step in range(1, n_col):
                total += pivot_split_in[col(step)]
            pivot_sum[...] = total
            for step in range(1, n_gz):
                pivot_sum_copy(step).start()

    def pivot_over_gz():
        @pl.when(r == 0)
        def _():
            for step in range(1, n_gz):
                remote(
                    pivot_sum, pivot_sum_in.at[gz(step)],
                    pivot_sum_send.at[0], pivot_sum_recv.at[gz(step)], gz=gz(step),
                ).wait_recv()
            total = pivot_sum[...]
            for step in range(1, n_gz):
                total += pivot_sum_in[gz(step)]
            pivot[c] = total
            for step in range(1, n_row):
                pivot_row_copy(step).start()

    def pivot_out():
        @pl.when(r != 0)
        def _():
            pivot_row_copy(1).wait_recv()

        for step in range(1, n_col):
            piece = pivot.at[c]
            start(remote(piece, piece, pivot_col_send.at[step], pivot_col_recv.at[c], col=col(step)))

    def pivot_done():
        for step in range(1, n_col):
            piece = pivot.at[col(step)]
            remote(
                piece, piece, pivot_col_send.at[0], pivot_col_recv.at[col(step)], col=col(step)
            ).wait_recv()
        whole = jnp.concatenate([pivot[at] for at in range(n_col)], axis=0)
        start_elimination(whole, worked, product, upper_unit)

    def chain(way, at):
        slot = 0 if way > 0 else 1
        piece = first_rows.at[pl.ds(at * (BLOCK // 2), BLOCK // 2), :]
        return remote(piece, piece, chain_send.at[slot, at], chain_recv.at[at], row=row(way))

    def chain_hop(hop):
        def pass_on(way):
            for at in range(2):
                chain(1, at).wait_recv()
                if way:
                    chain(way, at).start()

        @pl.when(r == hop)
        def _():
            pass_on(1 if hop < n_row // 2 else 0)

        if hop < n_row // 2:
            @pl.when(r == n_row - hop)
            def _():
                pass_on(-1 if hop < n_row // 2 - 1 else 0)

    def row_front_copy():
        return remote(
            front.at[pl.ds(0, BLOCK), :], row_front, row_front_sem.at[0], row_front_sem.at[1], row=g
        )

    def side(way):
        return pl.ds(0 if way > 0 else BLOCK, BLOCK)

    def up_arrive(step):
        block = gathered.at[0, col(step), :, side(1)]
        remote(uppers.at[0], block, up_send.at[0], up_recv.at[col(step)], col=col(step)).wait_recv()

    def z_wait(distance, way, place):
        k_block = col(ORDER_OF_K[place])
        slot = 0 if way > 0 else 1
        piece = gathered.at[distance, k_block, :, side(way)]
        remote(
            piece, piece, z_send.at[0, 0], z_recv.at[distance, slot, k_block], row=row(1)
        ).wait_recv()

    last = n_row // 2 - 1

    def ring_entry(way, at):
        def entry(order):
            away, place = order[at]
            if away == last and way < 0:
                place += n_col // 2
            return away, ORDER_OF_K[place]

        from_first = r if way > 0 else lax.rem(n_row - r, n_row)
        away, offset = entry(NATURAL)
        if all(entry(order) == (away, offset) for order in (RING if way > 0 else RING_BACK).values()):
            return away, offset
        for distance, order in (RING if way > 0 else RING_BACK).items():
            here = from_first == distance
            away = jnp.where(here, entry(order)[0], away)
            offset = jnp.where(here, entry(order)[1], offset)
        return away, offset

    def z_step(at):
        if 0 < at < n_col:
            up_arrive(ORDER_OF_K[at])
        for way in (1, -1):
            away, offset = ring_entry(way, at)
            k_block = col(offset)
            slot = 0 if way > 0 else 1
            lanes = side(way)
            if way < 0:
                start_lane = jnp.where(away == 0, 0, BLOCK)
                lanes = pl.ds(pl.multiple_of(start_lane, BLOCK), BLOCK)
            copy = remote(
                gathered.at[away, k_block, :, lanes], gathered.at[away + 1, k_block, :, side(way)],
                z_send.at[slot, at], z_recv.at[away + 1, slot, k_block], row=row(way),
            )
            arrived_here = gathered.at[away, k_block, :, lanes]
            arrival = remote(
                arrived_here, arrived_here, z_send.at[slot, at], z_recv.at[away, slot, k_block], row=row(way)
            )
            if not isinstance(away, int):
                pl.when(away > 0)(arrival.wait_recv)
            elif away > 0:
                arrival.wait_recv()
            start(copy)

    def far_wait(distance, way, places):
        @pl.when(row(-way * distance) != 0)
        def _():
            for place in places:
                z_wait(distance, way, place)

    def half_of(at):
        return pl.ds(at * half, half)

    def low_copy(way, second):
        slot = 0 if way > 0 else 1
        piece = lowers.at[c, half_of(1 - slot if second else slot), :]
        at = 4 + slot if second else slot
        return remote(piece, piece, low_send.at[at], low_recv.at[at], col=col(way))

    def low_start(second):
        for way in (1, -1):
            start(low_copy(way, second))

    def low_pass():
        for way in (1, -1):
            slot = 0 if way > 0 else 1
            piece = lowers.at[col(-way), half_of(slot), :]
            remote(piece, piece, low_send.at[slot], low_recv.at[slot], col=col(way)).wait_recv()
            start(remote(piece, piece, low_send.at[2 + slot], low_recv.at[2 + slot], col=col(way)))

    def low_done():
        for way in (1, -1):
            slot = 0 if way > 0 else 1
            piece = lowers.at[col(-way), half_of(1 - slot), :]
            remote(piece, piece, low_send.at[4 + slot], low_recv.at[4 + slot], col=col(way)).wait_recv()
            piece = lowers.at[col(2), half_of(slot), :]
            remote(piece, piece, low_send.at[2 + slot], low_recv.at[2 + slot], col=col(way)).wait_recv()

    def row_products():
        for at in range(n_col):
            split[at] = -jnp.dot(first_rows[...], uppers[at], preferred_element_type=jnp.float32)
        for step in range(1, n_col):
            start(
                remote(
                    split.at[col(step)], split_in.at[c],
                    split_send.at[step], split_recv.at[c], col=col(step),
                )
            )

    def row_copy():
        return remote(summed, row_in.at[g], row_send, row_recv.at[g], gz=r)

    def row_over_col():
        for step in range(1, n_col):
            remote(
                split.at[0], split_in.at[col(step)],
                split_send.at[0], split_recv.at[col(step)], col=col(step),
            ).wait_recv()
        total = split[c]
        for step in range(1, n_col):
            total += split_in[col(step)]
        summed[...] = total

        @pl.when(g != r)
        def _():
            row_copy().start()

    def spread_copy(step):
        return remote(row_panel, row_panel, spread_send.at[step], spread_recv, row=row(step))

    def row_over_gz():
        @pl.when(g == r)
        def _():
            @pl.when(g != 0)
            def _():
                row_front_copy().wait_recv()

            total = summed[...] + row_front[...]
            for step in range(1, n_gz):
                remote(
                    summed, row_in.at[gz(step)], row_send, row_recv.at[gz(step)], gz=gz(step)
                ).wait_recv()
                total += row_in[gz(step)]
            row_panel[...] = total
            for step in range(1, n_row):
                spread_copy(step).start()

    def strip_of(at):
        return pl.ds(pl.multiple_of(at * strip, strip), strip)

    def column_copy(step):
        return remote(
            column_part.at[strip_of(gz(step)), :], column_in.at[g],
            column_send.at[step], column_recv.at[g], gz=gz(step),
        )

    def hand_copy(step):
        piece = panel.at[strip_of(g), :]
        return remote(piece, piece, hand_send.at[step], hand_recv, col=col(step))

    def column_product():
        far = n_row // 2
        for plane, waits in (
            (far - 1, ((1, 2), (1, 3))),
            (far, ((1, 0), (1, 1), (-1, 2), (-1, 3))),
            (far + 1, ((-1, 0), (-1, 1))),
        ):
            @pl.when(r == plane)
            def _():
                for way, place in waits:
                    z_wait(min(plane, n_row - plane), way, place)

        distance = jnp.where(r <= far, r, n_row - r)

        def first_block(place):
            up = (r < far) | ((r == far) & (place < 2))
            lanes = pl.ds(pl.multiple_of(jnp.where(up, 0, BLOCK), BLOCK), BLOCK)
            return gathered[distance, col(ORDER_OF_K[place]), :, lanes]

        @pl.when(c == 0)
        def _():
            for which in range(2):
                column_part[which * half : (which + 1) * half, :] = -layer_rows(first_block, which)

            @pl.when(g == 0)
            def _():
                column_part[...] += front[...]

            for step in range(1, n_gz):
                column_copy(step).start()

    def column_over_gz():
        @pl.when(c == 0)
        def _():
            total = column_part[strip_of(g), :]
            for step in range(1, n_gz):
                remote(
                    column_part.at[strip_of(g), :], column_in.at[gz(step)],
                    column_send.at[0], column_recv.at[gz(step)], gz=gz(step),
                ).wait_recv()
                total += column_in[gz(step)]
            panel[strip_of(g), :] = total
            for step in range(1, n_col):
                hand_copy(step).start()

    def column_gather():
        @pl.when(c != 0)
        def _():
            hand_copy(1).wait_recv()

        piece = panel.at[strip_of(g), :]
        for step in range(1, n_gz):
            start(remote(piece, piece, panel_send.at[step], panel_recv.at[g], gz=gz(step)))

    def panel_done():
        for step in range(1, n_gz):
            piece = panel.at[strip_of(gz(step)), :]
            remote(piece, piece, panel_send.at[0], panel_recv.at[gz(step)], gz=gz(step)).wait_recv()

        @pl.when(g != r)
        def _():
            spread_copy(1).wait_recv()

    done = [0]

    def factor_part(count):
        eliminate(done[0], count, worked, product, upper_unit, lower_inverse)
        done[0] += count

    def term_copy(j):
        span = pl.ds(pl.multiple_of(core * half, half), half)
        return remote(terms.at[j], arrived.at[x, span, :], term_send.at[j], term_recv.at[g], gz=j)

    def layer_rows(block, which):
        span = pl.ds(which * half, half)
        if not isinstance(which, int):
            span = pl.ds(pl.multiple_of(which * half, half), half)
        total = None
        for place in range(n_col):
            k_block = col(ORDER_OF_K[place])
            part = jnp.dot(lowers[k_block, span, :], block(place), preferred_element_type=jnp.float32)
            total = part if total is None else total + part
        return total

    def pair_copy(j):
        return remote(pair_out.at[j], pair_in.at[j], pair_send.at[j], pair_recv.at[j], gz=sibling)

    def term(distance):
        def block(place):
            k_block = col(ORDER_OF_K[place])
            if 0 < distance <= last:
                return gathered[distance, k_block]
            return gathered[distance, k_block, :, side(1 if distance == 0 or place < 2 else -1)]

        ends = (row(-distance), row(distance)) if 0 < distance <= last else (row(distance),)

        def put(where, values, send):
            for at, j in enumerate(ends):
                @pl.when((j != 0) | (c != 0))
                def _():
                    where[j] = values[:, at * BLOCK : (at + 1) * BLOCK]
                    if send:
                        pair_copy(j).start()

        put(pair_out, layer_rows(block, 1 - core), True)
        put(terms, layer_rows(block, core), False)

    def term_out(distance):
        j = row(distance)

        @pl.when((j != 0) | (c != 0))
        def _():
            pair_copy(j).wait_recv()
            terms[j] += pair_in[j]

            @pl.when(j != g)
            def _():
                term_copy(j).start()

            @pl.when(j == g)
            def _():
                arrived[x, pl.ds(pl.multiple_of(core * half, half), half), :] = terms[j]

    @pl.when(r == 0)
    def _():
        for step in range(1, n_col):
            pivot_split_copy(step).start()
        for at in range(2):
            chain(1, at).start()
            chain(-1, at).start()

    for slot, step in enumerate(ORDER_OF_K[1:]):
        mine = gathered.at[0, c, :, side(1)]
        start(remote(uppers.at[col(step)], mine, up_send.at[slot], up_recv.at[c], col=col(step)))
    z_step(0)
    low_start(False)

    @pl.when((r == 0) & (g != 0))
    def _():
        row_front_copy().start()

    def panels_out(upper_inverse):
        panel_done()
        upper = exact_dot(lower_inverse[...], row_panel[...])
        upper_panel[...] = upper
        for at in range(panels):
            span = pl.ds(at * BLOCK, BLOCK)
            lower = exact_dot(panel[span, :], upper_inverse)
            lower_panel[span, :] = lower
            kept = jnp.where(corner, panel[span, :], front[span, :])
            trailing[span, :] = kept - exact_dot(lower, upper)

    def far_arrive():
        far_wait(last + 1, 1, (0, 1))
        far_wait(last + 1, -1, (2, 3))

    pivot_over_col()
    z_step(1)
    chain_hop(1)
    z_step(2)
    low_start(True)
    pivot_over_gz()
    z_step(3)
    chain_hop(2)
    z_step(4)
    pivot_out()
    low_pass()
    chain_hop(3)
    z_step(5)
    pivot_done()
    factor_part(8)
    chain_hop(4)
    row_products()
    factor_part(8)
    z_step(6)
    factor_part(8)
    z_step(7)
    row_over_col()
    factor_part(16)
    z_step(8)
    factor_part(16)
    z_step(9)
    row_over_gz()
    low_done()
    term(0)
    factor_part(8)
    z_step(10)
    column_product()
    term_out(0)
    factor_part(16)
    z_step(11)
    term(1)
    column_over_gz()
    term_out(1)
    term_out(-1)
    z_step(12)
    column_gather()
    factor_part(8)
    z_step(13)
    term(2)
    term_out(2)
    term_out(-2)
    far_wait(last, 1, (2, 3))
    far_wait(last, -1, (0, 1))
    term(3)
    term_out(3)
    term_out(-3)
    far_arrive()
    term(4)
    term_out(4)
    factor_part(40)
    upper_inverse = finish_elimination(worked, upper_unit)
    panels_out(upper_inverse)

    for copy in sends:
        copy.wait_send()
    for step in range(n_gz):
        j = gz(step)
        pl.when((j != 0) | (c != 0))(pair_copy(j).wait_send)

    @pl.when(c == 0)
    def _():
        for step in range(1, n_gz):
            column_copy(step).wait_send()
        for step in range(1, n_col):
            hand_copy(step).wait_send()

    @pl.when(r < n_row // 2)
    def _():
        for at in range(2):
            chain(1, at).wait_send()

    @pl.when((r == 0) | (r > n_row // 2 + 1))
    def _():
        for at in range(2):
            chain(-1, at).wait_send()

    @pl.when(r == 0)
    def _():
        for step in range(1, n_col):
            pivot_split_copy(step).wait_send()
        for step in range(1, n_gz):
            pivot_sum_copy(step).wait_send()
        for step in range(1, n_row):
            pivot_row_copy(step).wait_send()

    @pl.when((r == 0) & (g != 0))
    def _():
        row_front_copy().wait_send()

    @pl.when(g != r)
    def _():
        row_copy().wait_send()

    @pl.when(g == r)
    def _():
        for step in range(1, n_row):
            spread_copy(step).wait_send()

    @pl.when((g != 0) | (c != 0))
    def _():
        for step in range(1, n_gz):
            other = gz(step)
            span = pl.ds(pl.multiple_of(lax.rem(other, 2) * half, half), half)
            block = arrived.at[other // 2, span, :]
            remote(block, block, term_send.at[0], term_recv.at[other], gz=other).wait_recv()

        def add_up(at, carry):
            span = pl.ds(pl.multiple_of(at * BLOCK, BLOCK), BLOCK)
            total = arrived[0, span, :]
            for chip in range(1, n_gz // 2):
                total += arrived[chip, span, :]
            trailing[span, :] -= total
            return carry

        lax.fori_loop(0, panels, add_up, 0)

    for step in range(1, n_gz):
        j = gz(step)
        pl.when((j != 0) | (c != 0))(term_copy(j).wait_send)


def shards(n_gz, n_row, n_col, subtree_lower, subtree_upper, touched, front):
    height, depth = subtree_lower.shape[1:]
    width = front.shape[3]
    half = height // 2
    bf16, f32 = jnp.bfloat16, jnp.float32
    dma = pltpu.SemaphoreType.DMA
    backs = BLOCK // n_col
    vmem = pl.BlockSpec(memory_space=pltpu.VMEM)
    anywhere = pl.BlockSpec(memory_space=pltpu.HBM)
    lower_panel, upper_panel, trailing = pl.pallas_call(
        functools.partial(front_kernel, n_gz, n_row, n_col),
        out_shape=(
            jax.ShapeDtypeStruct((height, width), f32),
            jax.ShapeDtypeStruct((width, width), f32),
            jax.ShapeDtypeStruct((height, width), f32),
        ),
        in_specs=[anywhere] * 4,
        out_specs=(vmem, vmem, vmem),
        scratch_shapes=[
            pltpu.VMEM((height, depth), bf16),
            pltpu.VMEM((depth, height), bf16),
            pltpu.SMEM(touched.shape, jnp.int32),
            pltpu.VMEM((height, width), f32),
            pltpu.VMEM((n_col, height, depth), bf16),
            pltpu.VMEM((n_col, depth, BLOCK), bf16),
            pltpu.VMEM((n_row // 2 + 1, n_col, depth, 2 * BLOCK), bf16),
            pltpu.VMEM((n_gz, half, BLOCK), f32),
            pltpu.VMEM((n_gz, half, BLOCK), f32),
            pltpu.VMEM((n_gz, half, BLOCK), f32),
            pltpu.VMEM((n_gz // 2, height, BLOCK), f32),
            pltpu.VMEM((BLOCK, depth), bf16),
            pltpu.VMEM((BLOCK, BLOCK), f32),
            pltpu.VMEM((n_col, backs, BLOCK), f32),
            pltpu.VMEM((n_col, backs, BLOCK), f32),
            pltpu.VMEM((backs, BLOCK), f32),
            pltpu.VMEM((n_gz, backs, BLOCK), f32),
            pltpu.VMEM((n_col, backs, BLOCK), f32),
            pltpu.VMEM((n_col, BLOCK, BLOCK), f32),
            pltpu.VMEM((n_col, BLOCK, BLOCK), f32),
            pltpu.VMEM((BLOCK, BLOCK), f32),
            pltpu.VMEM((n_gz, BLOCK, BLOCK), f32),
            pltpu.VMEM((BLOCK, BLOCK), f32),
            pltpu.VMEM((height, BLOCK), f32),
            pltpu.VMEM((n_gz, height // n_gz, BLOCK), f32),
            pltpu.VMEM((height, BLOCK), f32),
            pltpu.VMEM((BLOCK, BLOCK), f32),
            pltpu.VMEM((BLOCK, BLOCK), f32),
            pltpu.VMEM((BLOCK, BLOCK), f32),
            pltpu.VMEM((BLOCK, BLOCK), f32),
            dma((4,)),
            dma((n_col,)), dma((n_col,)),
            dma((6,)), dma((6,)),
            dma((2, len(NATURAL))), dma((n_row // 2 + 1, 2, n_col)),
            dma((n_gz,)), dma((n_gz,)),
            dma((n_gz,)), dma((n_gz,)),
            dma((2, 2)), dma((2,)),
            dma((2,)),
            dma((n_col,)), dma((n_col,)),
            dma((n_gz,)), dma((n_gz,)),
            dma((n_row,)), dma,
            dma((n_col,)), dma((n_col,)),
            dma((n_col,)), dma((n_col,)),
            dma, dma((n_gz,)),
            dma((n_row,)), dma,
            dma((n_gz,)), dma((n_gz,)),
            dma((n_col,)), dma,
            dma((n_gz,)), dma((n_gz,)),
        ],
        compiler_params=pltpu.CompilerParams(
            collective_id=0, has_side_effects=True, vmem_limit_bytes=213 * 256 * 1024
        ),
    )(subtree_lower[0], subtree_upper[0], touched, front.reshape(height, width))
    return (
        lower_panel,
        upper_panel.reshape(width, 1, 1, width),
        trailing.reshape(height, 1, 1, width),
    )


def solution(mesh):
    placed = (
        P("gz", "row", "col"),
        P("gz", "col", "row"),
        P("gz", None),
        P("row", "gz", "col", None),
    )
    return jax.shard_map(
        functools.partial(shards, mesh.shape["gz"], mesh.shape["row"], mesh.shape["col"]),
        mesh=mesh,
        in_specs=placed,
        out_specs=(P("row", None), P(None, "gz", "col", None), P("row", "gz", "col", None)),
        check_vma=False,
    )
```

```python
import functools

import jax
import jax.numpy as jnp
from jax import lax
from jax.experimental import pallas as pl
from jax.experimental.pallas import tpu as pltpu
from jax.sharding import PartitionSpec as P

BLOCK = 128
GROUP = 4
MESH = pl.DeviceIdType.MESH
ORDER_OF_K = (0, 1, 3, 2)
NATURAL = [(away, place) for away in range(3) for place in range(4)] + [(3, 0), (3, 1)]
OWN, NEXT, FAR = NATURAL[0:4], NATURAL[4:8], NATURAL[8:12]
RING = {
    1: OWN[:2] + NEXT + OWN[2:] + FAR + [(3, 0), (3, 1)],
    2: OWN + FAR + NEXT + [(3, 0), (3, 1)],
    3: OWN + NEXT[:2] + [(3, 0), (3, 1)] + NEXT[2:] + FAR,
}
RING_BACK = {1: RING[1], 2: RING[2], 3: OWN + NEXT + [(3, 0), (3, 1)] + FAR}


def exact_dot(left, right):
    return jnp.dot(
        left, right, precision=lax.Precision.HIGHEST, preferred_element_type=jnp.float32
    )


def eliminate(first, count, worked, product, upper, lower_inverse):
    lanes = lax.broadcasted_iota(jnp.int32, (1, BLOCK), 1)
    rows = lax.broadcasted_iota(jnp.int32, (BLOCK, 1), 0)

    def step(group, carry):
        places = [group * GROUP + s for s in range(GROUP)]
        here = [lanes == place for place in places]
        dense, products, kept = worked[...], product[...], upper[...]
        pivot_rows = [worked[pl.ds(place, 1), :] for place in places]
        product_rows = [product[pl.ds(place, 1), :] for place in places]

        def take(values, hit):
            return jnp.sum(jnp.where(hit, values, 0.0), axis=1, keepdims=True)

        columns = [take(dense, hit) for hit in here]
        corner = [[take(line, hit) for hit in here] for line in pivot_rows]
        scaled = []
        for s in range(GROUP):
            inverse = 1.0 / corner[s][s]
            factors = jnp.where(rows == places[s], 0.0, columns[s] * inverse)
            for u in range(s + 1, GROUP):
                ratio = corner[u][s] * inverse
                pivot_rows[u] = pivot_rows[u] - ratio * pivot_rows[s]
                product_rows[u] = product_rows[u] - ratio * product_rows[s]
                for t in range(s + 1, GROUP):
                    corner[u][t] = corner[u][t] - ratio * corner[s][t]
            for t in range(s + 1, GROUP):
                columns[t] = columns[t] - factors * corner[s][t]
            scaled.append(factors)
        for s in range(GROUP):
            lower_inverse[pl.ds(places[s], 1), :] = product_rows[s]
            dense = dense - scaled[s] * pivot_rows[s]
            products = products - scaled[s] * product_rows[s]
            kept = jnp.where(here[s], -scaled[s], kept)
        worked[...] = dense
        product[...] = products
        upper[...] = kept
        return carry

    lax.fori_loop(first // GROUP, (first + count) // GROUP, step, 0)


def start_elimination(pivot, worked, product, upper):
    rows = lax.broadcasted_iota(jnp.int32, (BLOCK, BLOCK), 0)
    lanes = lax.broadcasted_iota(jnp.int32, (BLOCK, BLOCK), 1)
    identity = jnp.where(rows == lanes, 1.0, 0.0)
    worked[...] = pivot
    product[...] = identity
    upper[...] = identity


def finish_elimination(worked, upper):
    rows = lax.broadcasted_iota(jnp.int32, (BLOCK, BLOCK), 0)
    lanes = lax.broadcasted_iota(jnp.int32, (BLOCK, BLOCK), 1)
    pivots = jnp.sum(jnp.where(rows == lanes, worked[...], 0.0), axis=1, keepdims=True)
    unit = jnp.where(rows < lanes, upper[...], jnp.where(rows == lanes, 1.0, 0.0))
    return unit / pivots


def remote(src, dst, send_sem, recv_sem, **where):
    return pltpu.make_async_remote_copy(
        src_ref=src,
        dst_ref=dst,
        send_sem=send_sem,
        recv_sem=recv_sem,
        device_id=where,
        device_id_type=MESH,
    )


def front_kernel(
    n_gz, n_row, n_col,
    lower_hbm, upper_hbm, touched_hbm, front_hbm,
    lower_panel, upper_panel, trailing,
    lower_in, upper_in, touched, front,
    lowers, uppers, gathered, terms, pair_out, pair_in, arrived,
    first_rows, row_front,
    pivot_split, pivot_split_in, pivot_sum, pivot_sum_in, pivot,
    split, split_in, summed, row_in, row_panel, column_part, column_in, panel,
    worked, product, upper_unit, lower_inverse,
    in_sem, up_send, up_recv, low_send, low_recv, z_send, z_recv, term_send, term_recv,
    pair_send, pair_recv, chain_send, chain_recv, row_front_sem,
    pivot_split_send, pivot_split_recv, pivot_sum_send, pivot_sum_recv,
    pivot_row_send, pivot_row_recv, pivot_col_send, pivot_col_recv,
    split_send, split_recv, row_send, row_recv, spread_send, spread_recv,
    column_send, column_recv, hand_send, hand_recv, panel_send, panel_recv,
):
    g, r, c = lax.axis_index("gz"), lax.axis_index("row"), lax.axis_index("col")
    height = lower_in.shape[0]
    panels = height // BLOCK
    half = height // 2
    backs = BLOCK // n_col
    x, core = g // 2, lax.rem(g, 2)
    sibling = g + 1 - 2 * core
    sends = []

    def gz(step):
        return lax.rem(g + step, n_gz)

    def row(step):
        return lax.rem(r + n_row + step, n_row)

    def col(step):
        return lax.rem(c + n_col + step, n_col)

    def start(copy):
        copy.start()
        sends.append(copy)

    inputs = [
        pltpu.make_async_copy(upper_hbm, upper_in, in_sem.at[0]),
        pltpu.make_async_copy(touched_hbm, touched, in_sem.at[1]),
        pltpu.make_async_copy(lower_hbm, lower_in, in_sem.at[2]),
        pltpu.make_async_copy(front_hbm, front, in_sem.at[3]),
    ]
    for copy in inputs:
        copy.start()

    barrier = pltpu.get_barrier_semaphore()
    for step in range(1, n_gz):
        pl.semaphore_signal(barrier, inc=1, device_id={"gz": gz(step)}, device_id_type=MESH)
    for step in range(1, n_row):
        pl.semaphore_signal(barrier, inc=1, device_id={"row": row(step)}, device_id_type=MESH)
    for step in range(1, n_col):
        pl.semaphore_signal(barrier, inc=1, device_id={"col": col(step)}, device_id_type=MESH)

    for copy in inputs:
        copy.wait()
    for at in range(panels):
        mark = touched[0, r * panels + at].astype(jnp.float32)
        span = pl.ds(at * BLOCK, BLOCK)
        uppers[at] = (upper_in[:, span].astype(jnp.float32) * mark).astype(jnp.bfloat16)
        lowers[c, span, :] = (lower_in[span, :].astype(jnp.float32) * mark).astype(jnp.bfloat16)
    gathered[0, c, :, :BLOCK] = uppers[c]
    corner = (g == 0) & (c == 0)
    strip = height // n_gz

    @pl.when(r == 0)
    def _():
        first_rows[...] = lowers[c, :BLOCK, :]
        part = -jnp.dot(lowers[c, :BLOCK, :], uppers[0], preferred_element_type=jnp.float32)
        for at in range(n_col):
            pivot_split[at] = part[at * backs : (at + 1) * backs]

    @pl.when((r == 0) & (g == 0))
    def _():
        row_front[...] = front[:BLOCK, :]

    @pl.when((r == 0) & corner)
    def _():
        for at in range(n_col):
            pivot_split[at] += front[at * backs : (at + 1) * backs, :]

    pl.semaphore_wait(barrier, n_gz + n_row + n_col - 3)

    def pivot_split_copy(step):
        return remote(
            pivot_split.at[col(step)], pivot_split_in.at[c],
            pivot_split_send.at[step], pivot_split_recv.at[c], col=col(step),
        )

    def pivot_sum_copy(step):
        return remote(
            pivot_sum, pivot_sum_in.at[g], pivot_sum_send.at[step], pivot_sum_recv.at[g], gz=gz(step)
        )

    def pivot_row_copy(step):
        piece = pivot.at[c]
        return remote(piece, piece, pivot_row_send.at[step], pivot_row_recv, row=row(step))

    def pivot_over_col():
        @pl.when(r == 0)
        def _():
            for step in range(1, n_col):
                remote(
                    pivot_split.at[0], pivot_split_in.at[col(step)],
                    pivot_split_send.at[0], pivot_split_recv.at[col(step)], col=col(step),
                ).wait_recv()
            total = pivot_split[c]
            for step in range(1, n_col):
                total += pivot_split_in[col(step)]
            pivot_sum[...] = total
            for step in range(1, n_gz):
                pivot_sum_copy(step).start()

    def pivot_over_gz():
        @pl.when(r == 0)
        def _():
            for step in range(1, n_gz):
                remote(
                    pivot_sum, pivot_sum_in.at[gz(step)],
                    pivot_sum_send.at[0], pivot_sum_recv.at[gz(step)], gz=gz(step),
                ).wait_recv()
            total = pivot_sum[...]
            for step in range(1, n_gz):
                total += pivot_sum_in[gz(step)]
            pivot[c] = total
            for step in range(1, n_row):
                pivot_row_copy(step).start()

    def pivot_out():
        @pl.when(r != 0)
        def _():
            pivot_row_copy(1).wait_recv()

        for step in range(1, n_col):
            piece = pivot.at[c]
            start(remote(piece, piece, pivot_col_send.at[step], pivot_col_recv.at[c], col=col(step)))

    def pivot_done():
        for step in range(1, n_col):
            piece = pivot.at[col(step)]
            remote(
                piece, piece, pivot_col_send.at[0], pivot_col_recv.at[col(step)], col=col(step)
            ).wait_recv()
        whole = jnp.concatenate([pivot[at] for at in range(n_col)], axis=0)
        start_elimination(whole, worked, product, upper_unit)

    def chain(way, at):
        slot = 0 if way > 0 else 1
        piece = first_rows.at[pl.ds(at * (BLOCK // 2), BLOCK // 2), :]
        return remote(piece, piece, chain_send.at[slot, at], chain_recv.at[at], row=row(way))

    def chain_hop(hop):
        def pass_on(way):
            for at in range(2):
                chain(1, at).wait_recv()
                if way:
                    chain(way, at).start()

        @pl.when(r == hop)
        def _():
            pass_on(1 if hop < n_row // 2 else 0)

        if hop < n_row // 2:
            @pl.when(r == n_row - hop)
            def _():
                pass_on(-1 if hop < n_row // 2 - 1 else 0)

    def row_front_copy():
        return remote(
            front.at[pl.ds(0, BLOCK), :], row_front, row_front_sem.at[0], row_front_sem.at[1], row=g
        )

    def side(way):
        return pl.ds(0 if way > 0 else BLOCK, BLOCK)

    def up_arrive(step):
        block = gathered.at[0, col(step), :, side(1)]
        remote(uppers.at[0], block, up_send.at[0], up_recv.at[col(step)], col=col(step)).wait_recv()

    def z_wait(distance, way, place):
        k_block = col(ORDER_OF_K[place])
        slot = 0 if way > 0 else 1
        piece = gathered.at[distance, k_block, :, side(way)]
        remote(
            piece, piece, z_send.at[0, 0], z_recv.at[distance, slot, k_block], row=row(1)
        ).wait_recv()

    last = n_row // 2 - 1

    def ring_entry(way, at):
        def entry(order):
            away, place = order[at]
            if away == last and way < 0:
                place += n_col // 2
            return away, ORDER_OF_K[place]

        from_first = r if way > 0 else lax.rem(n_row - r, n_row)
        away, offset = entry(NATURAL)
        if all(entry(order) == (away, offset) for order in (RING if way > 0 else RING_BACK).values()):
            return away, offset
        for distance, order in (RING if way > 0 else RING_BACK).items():
            here = from_first == distance
            away = jnp.where(here, entry(order)[0], away)
            offset = jnp.where(here, entry(order)[1], offset)
        return away, offset

    def z_step(at):
        if 0 < at < n_col:
            up_arrive(ORDER_OF_K[at])
        for way in (1, -1):
            away, offset = ring_entry(way, at)
            k_block = col(offset)
            slot = 0 if way > 0 else 1
            lanes = side(way)
            if way < 0:
                start_lane = jnp.where(away == 0, 0, BLOCK)
                lanes = pl.ds(pl.multiple_of(start_lane, BLOCK), BLOCK)
            copy = remote(
                gathered.at[away, k_block, :, lanes], gathered.at[away + 1, k_block, :, side(way)],
                z_send.at[slot, at], z_recv.at[away + 1, slot, k_block], row=row(way),
            )
            arrived_here = gathered.at[away, k_block, :, lanes]
            arrival = remote(
                arrived_here, arrived_here, z_send.at[slot, at], z_recv.at[away, slot, k_block], row=row(way)
            )
            if not isinstance(away, int):
                pl.when(away > 0)(arrival.wait_recv)
            elif away > 0:
                arrival.wait_recv()
            start(copy)

    def far_wait(distance, way, places):
        @pl.when(row(-way * distance) != 0)
        def _():
            for place in places:
                z_wait(distance, way, place)

    def half_of(at):
        return pl.ds(at * half, half)

    def low_copy(way, second):
        slot = 0 if way > 0 else 1
        piece = lowers.at[c, half_of(1 - slot if second else slot), :]
        at = 4 + slot if second else slot
        return remote(piece, piece, low_send.at[at], low_recv.at[at], col=col(way))

    def low_start(second):
        for way in (1, -1):
            start(low_copy(way, second))

    def low_pass():
        for way in (1, -1):
            slot = 0 if way > 0 else 1
            piece = lowers.at[col(-way), half_of(slot), :]
            remote(piece, piece, low_send.at[slot], low_recv.at[slot], col=col(way)).wait_recv()
            start(remote(piece, piece, low_send.at[2 + slot], low_recv.at[2 + slot], col=col(way)))

    def low_done():
        for way in (1, -1):
            slot = 0 if way > 0 else 1
            piece = lowers.at[col(-way), half_of(1 - slot), :]
            remote(piece, piece, low_send.at[4 + slot], low_recv.at[4 + slot], col=col(way)).wait_recv()
            piece = lowers.at[col(2), half_of(slot), :]
            remote(piece, piece, low_send.at[2 + slot], low_recv.at[2 + slot], col=col(way)).wait_recv()

    def row_products():
        for at in range(n_col):
            split[at] = -jnp.dot(first_rows[...], uppers[at], preferred_element_type=jnp.float32)
        for step in range(1, n_col):
            start(
                remote(
                    split.at[col(step)], split_in.at[c],
                    split_send.at[step], split_recv.at[c], col=col(step),
                )
            )

    def row_copy():
        return remote(summed, row_in.at[g], row_send, row_recv.at[g], gz=r)

    def row_over_col():
        for step in range(1, n_col):
            remote(
                split.at[0], split_in.at[col(step)],
                split_send.at[0], split_recv.at[col(step)], col=col(step),
            ).wait_recv()
        total = split[c]
        for step in range(1, n_col):
            total += split_in[col(step)]
        summed[...] = total

        @pl.when(g != r)
        def _():
            row_copy().start()

    def spread_copy(step):
        return remote(row_panel, row_panel, spread_send.at[step], spread_recv, row=row(step))

    def row_over_gz():
        @pl.when(g == r)
        def _():
            @pl.when(g != 0)
            def _():
                row_front_copy().wait_recv()

            total = summed[...] + row_front[...]
            for step in range(1, n_gz):
                remote(
                    summed, row_in.at[gz(step)], row_send, row_recv.at[gz(step)], gz=gz(step)
                ).wait_recv()
                total += row_in[gz(step)]
            row_panel[...] = total
            for step in range(1, n_row):
                spread_copy(step).start()

    def strip_of(at):
        return pl.ds(pl.multiple_of(at * strip, strip), strip)

    def column_copy(step):
        return remote(
            column_part.at[strip_of(gz(step)), :], column_in.at[g],
            column_send.at[step], column_recv.at[g], gz=gz(step),
        )

    def hand_copy(step):
        piece = panel.at[strip_of(g), :]
        return remote(piece, piece, hand_send.at[step], hand_recv, col=col(step))

    def column_product():
        far = n_row // 2
        for plane, waits in (
            (far - 1, ((1, 2), (1, 3))),
            (far, ((1, 0), (1, 1), (-1, 2), (-1, 3))),
            (far + 1, ((-1, 0), (-1, 1))),
        ):
            @pl.when(r == plane)
            def _():
                for way, place in waits:
                    z_wait(min(plane, n_row - plane), way, place)

        distance = jnp.where(r <= far, r, n_row - r)

        def first_block(place):
            up = (r < far) | ((r == far) & (place < 2))
            lanes = pl.ds(pl.multiple_of(jnp.where(up, 0, BLOCK), BLOCK), BLOCK)
            return gathered[distance, col(ORDER_OF_K[place]), :, lanes]

        @pl.when(c == 0)
        def _():
            for which in range(2):
                column_part[which * half : (which + 1) * half, :] = -layer_rows(first_block, which)

            @pl.when(g == 0)
            def _():
                column_part[...] += front[...]

            for step in range(1, n_gz):
                column_copy(step).start()

    def column_over_gz():
        @pl.when(c == 0)
        def _():
            total = column_part[strip_of(g), :]
            for step in range(1, n_gz):
                remote(
                    column_part.at[strip_of(g), :], column_in.at[gz(step)],
                    column_send.at[0], column_recv.at[gz(step)], gz=gz(step),
                ).wait_recv()
                total += column_in[gz(step)]
            panel[strip_of(g), :] = total
            for step in range(1, n_col):
                hand_copy(step).start()

    def column_gather():
        @pl.when(c != 0)
        def _():
            hand_copy(1).wait_recv()

        piece = panel.at[strip_of(g), :]
        for step in range(1, n_gz):
            start(remote(piece, piece, panel_send.at[step], panel_recv.at[g], gz=gz(step)))

    def panel_done():
        for step in range(1, n_gz):
            piece = panel.at[strip_of(gz(step)), :]
            remote(piece, piece, panel_send.at[0], panel_recv.at[gz(step)], gz=gz(step)).wait_recv()

        @pl.when(g != r)
        def _():
            spread_copy(1).wait_recv()

    done = [0]

    def factor_part(count):
        eliminate(done[0], count, worked, product, upper_unit, lower_inverse)
        done[0] += count

    def term_copy(j):
        span = pl.ds(pl.multiple_of(core * half, half), half)
        return remote(terms.at[j], arrived.at[x, span, :], term_send.at[j], term_recv.at[g], gz=j)

    def layer_rows(block, which):
        span = pl.ds(which * half, half)
        if not isinstance(which, int):
            span = pl.ds(pl.multiple_of(which * half, half), half)
        total = None
        for place in range(n_col):
            k_block = col(ORDER_OF_K[place])
            part = jnp.dot(lowers[k_block, span, :], block(place), preferred_element_type=jnp.float32)
            total = part if total is None else total + part
        return total

    def pair_copy(j):
        return remote(pair_out.at[j], pair_in.at[j], pair_send.at[j], pair_recv.at[j], gz=sibling)

    def term(distance):
        def block(place):
            k_block = col(ORDER_OF_K[place])
            if 0 < distance <= last:
                return gathered[distance, k_block]
            return gathered[distance, k_block, :, side(1 if distance == 0 or place < 2 else -1)]

        ends = (row(-distance), row(distance)) if 0 < distance <= last else (row(distance),)

        def put(where, values, send):
            for at, j in enumerate(ends):
                @pl.when((j != 0) | (c != 0))
                def _():
                    where[j] = values[:, at * BLOCK : (at + 1) * BLOCK]
                    if send:
                        pair_copy(j).start()

        put(pair_out, layer_rows(block, 1 - core), True)
        put(terms, layer_rows(block, core), False)

    def term_out(distance):
        j = row(distance)

        @pl.when((j != 0) | (c != 0))
        def _():
            pair_copy(j).wait_recv()
            terms[j] += pair_in[j]

            @pl.when(j != g)
            def _():
                term_copy(j).start()

            @pl.when(j == g)
            def _():
                arrived[x, pl.ds(pl.multiple_of(core * half, half), half), :] = terms[j]

    for slot, step in enumerate(ORDER_OF_K[1:]):
        mine = gathered.at[0, c, :, side(1)]
        start(remote(uppers.at[col(step)], mine, up_send.at[slot], up_recv.at[c], col=col(step)))
    @pl.when(r == 0)
    def _():
        for step in range(1, n_col):
            pivot_split_copy(step).start()
        for at in range(2):
            chain(1, at).start()
            chain(-1, at).start()

    z_step(0)
    low_start(False)

    @pl.when((r == 0) & (g != 0))
    def _():
        row_front_copy().start()

    def panels_out(upper_inverse):
        panel_done()
        upper = exact_dot(lower_inverse[...], row_panel[...])
        upper_panel[...] = upper
        for at in range(panels):
            span = pl.ds(at * BLOCK, BLOCK)
            lower = exact_dot(panel[span, :], upper_inverse)
            lower_panel[span, :] = lower
            kept = jnp.where(corner, panel[span, :], front[span, :])
            trailing[span, :] = kept - exact_dot(lower, upper)

    def far_arrive():
        far_wait(last + 1, 1, (0, 1))
        far_wait(last + 1, -1, (2, 3))

    pivot_over_col()
    z_step(1)
    chain_hop(1)
    z_step(2)
    low_start(True)
    pivot_over_gz()
    z_step(3)
    chain_hop(2)
    z_step(4)
    pivot_out()
    low_pass()
    chain_hop(3)
    z_step(5)
    pivot_done()
    factor_part(8)
    chain_hop(4)
    row_products()
    factor_part(8)
    z_step(6)
    factor_part(8)
    z_step(7)
    row_over_col()
    factor_part(16)
    z_step(8)
    factor_part(16)
    z_step(9)
    row_over_gz()
    low_done()
    term(0)
    factor_part(8)
    z_step(10)
    column_product()
    term_out(0)
    factor_part(16)
    z_step(11)
    term(1)
    column_over_gz()
    term_out(1)
    term_out(-1)
    z_step(12)
    column_gather()
    factor_part(8)
    z_step(13)
    term(2)
    term_out(2)
    term_out(-2)
    far_wait(last, 1, (2, 3))
    far_wait(last, -1, (0, 1))
    term(3)
    term_out(3)
    term_out(-3)
    far_arrive()
    term(4)
    term_out(4)
    factor_part(40)
    upper_inverse = finish_elimination(worked, upper_unit)
    panels_out(upper_inverse)

    for copy in sends:
        copy.wait_send()
    for step in range(n_gz):
        j = gz(step)
        pl.when((j != 0) | (c != 0))(pair_copy(j).wait_send)

    @pl.when(c == 0)
    def _():
        for step in range(1, n_gz):
            column_copy(step).wait_send()
        for step in range(1, n_col):
            hand_copy(step).wait_send()

    @pl.when(r < n_row // 2)
    def _():
        for at in range(2):
            chain(1, at).wait_send()

    @pl.when((r == 0) | (r > n_row // 2 + 1))
    def _():
        for at in range(2):
            chain(-1, at).wait_send()

    @pl.when(r == 0)
    def _():
        for step in range(1, n_col):
            pivot_split_copy(step).wait_send()
        for step in range(1, n_gz):
            pivot_sum_copy(step).wait_send()
        for step in range(1, n_row):
            pivot_row_copy(step).wait_send()

    @pl.when((r == 0) & (g != 0))
    def _():
        row_front_copy().wait_send()

    @pl.when(g != r)
    def _():
        row_copy().wait_send()

    @pl.when(g == r)
    def _():
        for step in range(1, n_row):
            spread_copy(step).wait_send()

    @pl.when((g != 0) | (c != 0))
    def _():
        for step in range(1, n_gz):
            other = gz(step)
            span = pl.ds(pl.multiple_of(lax.rem(other, 2) * half, half), half)
            block = arrived.at[other // 2, span, :]
            remote(block, block, term_send.at[0], term_recv.at[other], gz=other).wait_recv()

        def add_up(at, carry):
            span = pl.ds(pl.multiple_of(at * BLOCK, BLOCK), BLOCK)
            total = arrived[0, span, :]
            for chip in range(1, n_gz // 2):
                total += arrived[chip, span, :]
            trailing[span, :] -= total
            return carry

        lax.fori_loop(0, panels, add_up, 0)

    for step in range(1, n_gz):
        j = gz(step)
        pl.when((j != 0) | (c != 0))(term_copy(j).wait_send)


def shards(n_gz, n_row, n_col, subtree_lower, subtree_upper, touched, front):
    height, depth = subtree_lower.shape[1:]
    width = front.shape[3]
    half = height // 2
    bf16, f32 = jnp.bfloat16, jnp.float32
    dma = pltpu.SemaphoreType.DMA
    backs = BLOCK // n_col
    vmem = pl.BlockSpec(memory_space=pltpu.VMEM)
    anywhere = pl.BlockSpec(memory_space=pltpu.HBM)
    lower_panel, upper_panel, trailing = pl.pallas_call(
        functools.partial(front_kernel, n_gz, n_row, n_col),
        out_shape=(
            jax.ShapeDtypeStruct((height, width), f32),
            jax.ShapeDtypeStruct((width, width), f32),
            jax.ShapeDtypeStruct((height, width), f32),
        ),
        in_specs=[anywhere] * 4,
        out_specs=(vmem, vmem, vmem),
        scratch_shapes=[
            pltpu.VMEM((height, depth), bf16),
            pltpu.VMEM((depth, height), bf16),
            pltpu.SMEM(touched.shape, jnp.int32),
            pltpu.VMEM((height, width), f32),
            pltpu.VMEM((n_col, height, depth), bf16),
            pltpu.VMEM((n_col, depth, BLOCK), bf16),
            pltpu.VMEM((n_row // 2 + 1, n_col, depth, 2 * BLOCK), bf16),
            pltpu.VMEM((n_gz, half, BLOCK), f32),
            pltpu.VMEM((n_gz, half, BLOCK), f32),
            pltpu.VMEM((n_gz, half, BLOCK), f32),
            pltpu.VMEM((n_gz // 2, height, BLOCK), f32),
            pltpu.VMEM((BLOCK, depth), bf16),
            pltpu.VMEM((BLOCK, BLOCK), f32),
            pltpu.VMEM((n_col, backs, BLOCK), f32),
            pltpu.VMEM((n_col, backs, BLOCK), f32),
            pltpu.VMEM((backs, BLOCK), f32),
            pltpu.VMEM((n_gz, backs, BLOCK), f32),
            pltpu.VMEM((n_col, backs, BLOCK), f32),
            pltpu.VMEM((n_col, BLOCK, BLOCK), f32),
            pltpu.VMEM((n_col, BLOCK, BLOCK), f32),
            pltpu.VMEM((BLOCK, BLOCK), f32),
            pltpu.VMEM((n_gz, BLOCK, BLOCK), f32),
            pltpu.VMEM((BLOCK, BLOCK), f32),
            pltpu.VMEM((height, BLOCK), f32),
            pltpu.VMEM((n_gz, height // n_gz, BLOCK), f32),
            pltpu.VMEM((height, BLOCK), f32),
            pltpu.VMEM((BLOCK, BLOCK), f32),
            pltpu.VMEM((BLOCK, BLOCK), f32),
            pltpu.VMEM((BLOCK, BLOCK), f32),
            pltpu.VMEM((BLOCK, BLOCK), f32),
            dma((4,)),
            dma((n_col,)), dma((n_col,)),
            dma((6,)), dma((6,)),
            dma((2, len(NATURAL))), dma((n_row // 2 + 1, 2, n_col)),
            dma((n_gz,)), dma((n_gz,)),
            dma((n_gz,)), dma((n_gz,)),
            dma((2, 2)), dma((2,)),
            dma((2,)),
            dma((n_col,)), dma((n_col,)),
            dma((n_gz,)), dma((n_gz,)),
            dma((n_row,)), dma,
            dma((n_col,)), dma((n_col,)),
            dma((n_col,)), dma((n_col,)),
            dma, dma((n_gz,)),
            dma((n_row,)), dma,
            dma((n_gz,)), dma((n_gz,)),
            dma((n_col,)), dma,
            dma((n_gz,)), dma((n_gz,)),
        ],
        compiler_params=pltpu.CompilerParams(
            collective_id=0, has_side_effects=True, vmem_limit_bytes=213 * 256 * 1024
        ),
    )(subtree_lower[0], subtree_upper[0], touched, front.reshape(height, width))
    return (
        lower_panel,
        upper_panel.reshape(width, 1, 1, width),
        trailing.reshape(height, 1, 1, width),
    )


def solution(mesh):
    placed = (
        P("gz", "row", "col"),
        P("gz", "col", "row"),
        P("gz", None),
        P("row", "gz", "col", None),
    )
    return jax.shard_map(
        functools.partial(shards, mesh.shape["gz"], mesh.shape["row"], mesh.shape["col"]),
        mesh=mesh,
        in_specs=placed,
        out_specs=(P("row", None), P(None, "gz", "col", None), P("row", "gz", "col", None)),
        check_vma=False,
    )
```
